256 devices in a mesh: lev: 8 (over y, z_hi), gy: 4 (over x), gx: 8 (over z_lo, core).
Axes of the slice: x: 4, y: 4, z: 8 (z_hi: 2, z_lo: 4; z = z_hi * 4 + z_lo), core: 2. Of those that a mesh axis runs over, the one named last changes fastest.
Arguments:
- fields: bfloat16 [320, 256, 2048], P('lev', 'gy', 'gx'), may hold values from -6 to 6
- sea_mask: int32 [256, 2048], P('gy', 'gx'), may hold values 0 or 1
- fold_partner: int32 [2048], replicated, may hold values from 0 to 2047, as said below
- embed_weight: bfloat16 [320, 192], P('lev'), may hold values from -0.3125 to 0.3125
- dw_weight: float32 [2, 192, 7, 7], P(None, 'lev'), may hold values from -0.875 to 0.875
- ln_gain: bfloat16 [2, 192], P(None, 'lev'), may hold values from 0.099609375 to 1.8984375
- up_weight: bfloat16 [2, 768, 192], P(None, 'lev'), may hold values from -0.4375 to 0.4375
- down_weight: bfloat16 [2, 768, 192], P(None, 'lev'), may hold values from -0.21875 to 0.21875
Outputs:
- encoded: bfloat16 [192, 256, 2048], P('lev', 'gy', 'gx')
The draws below stay inside these ranges and needn't reach their ends.
Inputs may be any that keep to these rules, and one draw needn't show every extreme that they name: fold_partner[fold_partner[i]] = i: the columns pair up across the north fold.
All inputs are finite; a program needn't handle non-finite values. No bound on the sum of `sea_mask` on one device may be relied on, other than what follows from the above.
Results may differ from the reference program's by a relative error of at most 0.027.
Values may be sent and summed in bfloat16 or wider, within the bound.
A program may use at most 64 MiB of HBM per device.

```python
import jax
import jax.numpy as jnp
from jax import lax

C = 192
HID = 768
BLOCKS = 2
C_IN = 320
NY = 256
NX = 2048
N_LEV = 8


def draw_fold_partner(key, part):
    key = jax.random.fold_in(key, 7)
    offset = jax.random.randint(key, (), 0, NX, dtype=jnp.int32)
    columns = jnp.arange(NX, dtype=jnp.int32)
    return jnp.mod(offset - columns, NX).astype(jnp.int32)


def touch_ends(result, stream_key, smallest, top_value):
    place = [jax.random.randint(jax.random.fold_in(stream_key, axis), (), 0, length) for axis, length in enumerate(result.shape)]
    widest = result.shape.index(max(result.shape))
    neighbour = place[:widest] + [(place[widest] + 1) % result.shape[widest]] + place[widest + 1:]
    return result.at[tuple(place)].set(smallest).at[tuple(neighbour)].set(top_value)


def shard_levels(stream_key, extent, shards, low, largest):
    loudness, own = 1.0, jax.random.fold_in(stream_key, 6)
    for dim, parts in shards:
        draws = jnp.exp(jax.random.uniform(jax.random.fold_in(own, dim), (parts,), jnp.float32, low / len(shards), largest / len(shards)))
        loudness = loudness * jnp.repeat(draws, extent[dim] // parts).reshape([-1 if axis == dim else 1 for axis in range(len(extent))])
    return loudness


def noise(rng, extent, deviation, limit, split=(), held_as=jnp.bfloat16):
    level = shard_levels(rng, extent, split, -0.22, 0.18) if split else 1.0
    entries = jax.random.normal(rng, extent, jnp.float32) * deviation * level
    return jnp.minimum(jnp.maximum(entries, -limit), limit).astype(held_as)


def setup_inputs(seed: int = 0) -> dict:
    splits = jax.random.split(jax.random.key(seed), 9)
    return {
        "fields": noise(splits[0], (C_IN, NY, NX), 1.0, 6.0, ((0, 8), (1, 4), (2, 8))),
        "sea_mask": touch_ends((jax.random.randint(splits[1], (NY, NX), 0, 4) < 3).astype(jnp.int32), jax.random.fold_in(splits[1], 1), 0, 1),
        "fold_partner": draw_fold_partner(jax.random.fold_in(splits[8], 71), 0),
        "embed_weight": noise(splits[3], (C_IN, C), C_IN ** -0.5, 0.3125, ((0, 8),)),
        "dw_weight": noise(splits[4], (BLOCKS, C, 7, 7), 49 ** -0.5, 0.875, ((1, 8),), jnp.float32),
        "ln_gain": jnp.clip(1.0 + 0.18 * jax.random.normal(splits[5], (BLOCKS, C), jnp.float32), 0.099609375, 1.8984375).astype(jnp.bfloat16),
        "up_weight": noise(splits[6], (BLOCKS, HID, C), C ** -0.5, 0.4375, ((1, 8),)),
        "down_weight": noise(splits[7], (BLOCKS, HID, C), HID ** -0.5, 0.21875, ((1, 8),)),
    }


def pad_field(state, fold_partner):
    top = state[:, NY - 3:, :][:, ::-1, :][:, :, fold_partner]
    bottom = jnp.zeros((state.shape[0], 3, NX), state.dtype)
    rows = jnp.concatenate([bottom, state, top], axis=1)
    return jnp.concatenate([rows[:, :, NX - 3:], rows, rows[:, :, :3]], axis=2)

def depthwise(padded, kernel):
    height = padded.shape[1] - 6
    width = padded.shape[2] - 6
    total = jnp.zeros((padded.shape[0], height, width), jnp.float32)
    for row_off in range(7):
        for col_off in range(7):
            tap = kernel[:, row_off, col_off][:, None, None]
            total = total + tap * padded[:, row_off:row_off + height, col_off:col_off + width].astype(jnp.float32)
    return total

def reference(fields, sea_mask, fold_partner, embed_weight, dw_weight, ln_gain, up_weight, down_weight):
    sea = sea_mask.astype(jnp.float32)
    cells = NY * NX
    flat = fields.reshape(C_IN, cells)
    group_in = C_IN // N_LEV
    total = jnp.zeros((C, cells), jnp.float32)
    for group in range(N_LEV):
        part = lax.dot_general(embed_weight[group * group_in:(group + 1) * group_in], flat[group * group_in:(group + 1) * group_in], (((0,), (0,)), ((), ())), preferred_element_type=jnp.float32)
        total = total + part.astype(jnp.bfloat16).astype(jnp.float32)
    state = (sea * total.reshape(C, NY, NX)).astype(jnp.bfloat16)
    group_hid = HID // N_LEV
    for block in range(BLOCKS):
        padded = pad_field(state, fold_partner)
        conv = depthwise(padded, dw_weight[block])
        mean_val = lax.optimization_barrier(jnp.mean(conv, axis=0))
        var_val = lax.optimization_barrier(jnp.mean(conv * conv, axis=0)) - mean_val * mean_val
        gain = ln_gain[block].astype(jnp.float32)[:, None, None]
        normed = ((conv - mean_val) * lax.rsqrt(var_val + 1e-06) * gain).astype(jnp.bfloat16)
        normed_flat = normed.reshape(C, cells)
        branch = jnp.zeros((C, cells), jnp.float32)
        for group in range(N_LEV):
            pre = jnp.dot(up_weight[block, group * group_hid:(group + 1) * group_hid], normed_flat, preferred_element_type=jnp.float32)
            hidden = jax.nn.gelu(pre, approximate=True).astype(jnp.bfloat16)
            part = lax.dot_general(down_weight[block, group * group_hid:(group + 1) * group_hid], hidden, (((0,), (0,)), ((), ())), preferred_element_type=jnp.float32)
            branch = branch + part.astype(jnp.bfloat16).astype(jnp.float32)
        state = (sea * (state.astype(jnp.float32) + branch.reshape(C, NY, NX))).astype(jnp.bfloat16)
    return state
```

```python
import jax
import jax.numpy as jnp
from jax import lax
from jax.experimental import pallas as pl
from jax.experimental.pallas import tpu as pltpu
from jax.sharding import PartitionSpec as P

BF = jnp.bfloat16
F32 = jnp.float32
MESH = pl.DeviceIdType.MESH
GROUPS = 12


def device(x, y, z, c):
    return (y * 2 + z // 4, x, lax.rem(z, 4) * 2 + c)


def kernel(
    fields, sea, partner, embed, dwg, up, down,
    out,
    x_in, mask_in, xt, flat, pe, dw_in, dw_all, emb_t, w_own, w_other, down_t, gain, conv,
    state, south, north, pack_e, pack_w, from_w, from_e, xrow, srow,
    fold_in, fold_out, out_f, out_b,
    s_x, r_x, s_m, r_m, s_loc, s_w, r_w, s_halo, r_halo, s_f1, r_f1, s_f3, r_f3, s_o, r_o,
):
    lev = lax.axis_index("lev")
    x = lax.axis_index("gy")
    gx = lax.axis_index("gx")
    y = lev // 2
    z = lax.rem(lev, 2) * 4 + gx // 2
    c = lax.rem(gx, 2)

    def row_block(yy):
        return jnp.where(lax.rem(x, 2) == 0, yy, 3 - yy)

    def is_b(zz):
        return jnp.where((zz >= 2) & (zz <= 5), 0, 1)

    def half(zz):
        return lax.rem(is_b(zz) + c, 2)

    def hop(zz, k):
        return lax.rem(zz + k + 8, 8)

    rb = row_block(y)
    b_side = is_b(z)
    s = half(z)
    t = lax.rem(z + 2, 4)
    col_block = (t * 2 + c) * 2 + s
    line = z * 2 + c
    on_line = (x == 3) & (rb == 3)
    has_south = jnp.logical_not((x == 0) & (rb == 0))
    has_north = jnp.logical_not(on_line)

    far = hop(z, 4)
    same_chip = b_side == 1
    east_z = jnp.where(b_side == 0, jnp.where(c == 0, far, 2 + lax.rem(t + 1, 4)), jnp.where(c == 0, z, far))
    east_c = jnp.where(b_side == 0, 0, 1)
    west_z = jnp.where(b_side == 0, jnp.where(c == 1, far, 2 + lax.rem(t + 3, 4)), jnp.where(c == 1, z, far))
    west_c = jnp.where(b_side == 0, 1, 0)
    east = device(x, y, east_z, east_c)
    west = device(x, y, west_z, west_c)
    x_even = lax.rem(x, 2) == 0
    step = jnp.where(x_even, 1, -1)
    north_x = jnp.where(rb == 3, jnp.minimum(x + 1, 3), x)
    north_y = jnp.where(rb == 3, y, jnp.clip(y + step, 0, 3))
    south_x = jnp.where(rb == 0, jnp.maximum(x - 1, 0), x)
    south_y = jnp.where(rb == 0, y, jnp.clip(y - step, 0, 3))
    north_dev = device(north_x, north_y, z, c)
    south_dev = device(south_x, south_y, z, c)

    def remote(src, dst, send, recv, dev):
        return pltpu.make_async_remote_copy(
            src_ref=src, dst_ref=dst, send_sem=send, recv_sem=recv, device_id=dev, device_id_type=MESH
        )

    ys = [lax.rem(y + k, 4) for k in range(4)]

    barrier = pltpu.get_barrier_semaphore()
    peers = [device(x, yy, hop(z, d), c) for d in (2, -2) for yy in ys]
    peers += [device(x, yy, z, c) for yy in ys[1:]]
    peers += [device(x, y, far, c)]
    peers += [device(lax.rem(x + k, 4), y, z, c) for k in (1, 2, 3)]
    peers += [device(x, y, z, 1 - c)]

    def greet(dev):
        pl.semaphore_signal(barrier, inc=1, device_id=dev, device_id_type=MESH)

    for dev in peers:
        greet(dev)

    @pl.when(on_line)
    def _():
        for k in range(1, 8):
            greet(device(x, y, hop(z, k), 1 - c))
            if k % 2:
                greet(device(x, y, hop(z, k), c))

    @pl.when(has_north & (b_side == 0))
    def _():
        greet(device(x, y, jnp.where(c == 0, west_z, east_z), 1 - c))

    slot = pe.at[y, lax.rem(lev, 2)]
    dslot = dw_in.at[y, lax.rem(lev, 2)]
    half_rows = pl.ds(pl.multiple_of(c * 48, 16), 48)
    for k, ref in enumerate((up.at[0], down.at[0], up.at[1], down.at[1])):
        @pl.when(x == k)
        def _():
            pltpu.make_async_copy(ref.at[half_rows, :], slot.at[0], s_loc.at[0]).start()
    pltpu.make_async_copy(embed, slot.at[1], s_loc.at[1]).start()
    pltpu.make_async_copy(dwg, dslot, s_loc.at[2]).start()

    pl.semaphore_wait(barrier, len(peers) + jnp.where(on_line, 11, 1 - b_side))

    pltpu.make_async_copy(up.at[0].at[half_rows, :], slot.at[0], s_loc.at[0]).wait()
    pltpu.make_async_copy(embed, slot.at[1], s_loc.at[1]).wait()
    pltpu.make_async_copy(dwg, dslot, s_loc.at[2]).wait()

    far_dev = device(x, y, far, c)
    w1 = remote(slot, slot, s_w.at[0], r_w.at[0], far_dev)
    w1.start()
    d1 = remote(dslot, dslot, s_w.at[1], r_w.at[1], far_dev)
    d1.start()

    def cells_of(yy, zz):
        return (
            pl.ds(pl.multiple_of(row_block(yy) * 16, 16), 16),
            pl.ds(pl.multiple_of(half(zz) * 128, 128), 128),
        )

    sends = []
    z_up = hop(z, 2)
    mrows, mcols = cells_of(y, z_up)
    m_copy = remote(sea.at[mrows, mcols], mask_in, s_m, r_m, device(x, y, z_up, c))
    m_copy.start()
    for k, yy in enumerate(ys):
        for j, d in enumerate((2, -2)):
            zz = hop(z, d)
            rows, cols = cells_of(yy, zz)
            cp = remote(
                fields.at[:, rows, cols], x_in.at[lev], s_x.at[2 * k + j], r_x.at[lev], device(x, yy, zz, c)
            )
            cp.start()
            sends.append(cp)

    def arrived(dst, sem):
        remote(dst, dst, s_m, sem, far_dev).wait_recv()

    arrived(pe.at[y, 1 - lax.rem(lev, 2)], r_w.at[0])
    arrived(dw_in.at[y, 1 - lax.rem(lev, 2)], r_w.at[1])
    for k in (1, 2, 3):
        dev = device(x, ys[k], z, c)
        cp = remote(pe.at[y], pe.at[y], s_w.at[2 * k], r_w.at[2 + y], dev)
        cp.start()
        sends.append(cp)
        cp = remote(dw_in.at[y], dw_in.at[y], s_w.at[2 * k + 1], r_w.at[6 + y], dev)
        cp.start()
        sends.append(cp)
    for k in (1, 2, 3):
        arrived(pe.at[ys[k]], r_w.at[2 + ys[k]])
        arrived(dw_in.at[ys[k]], r_w.at[6 + ys[k]])

    for k in (1, 2, 3):
        cp = remote(
            pe.at[:, :, 0], w_own.at[x], s_w.at[7 + k], r_w.at[10 + x], device(lax.rem(x + k, 4), y, z, c)
        )
        cp.start()
        sends.append(cp)
    w_own[x] = pe[:, :, 0]
    for l in range(8):
        for b in range(2):
            dw_all[b, l * 24 : (l + 1) * 24, :] = dw_in[l // 2, l % 2, b]
    for b in range(2):
        gain[b] = jnp.broadcast_to(dw_all[b, :, 49:50], (192, 128))
    emb_t[...] = pe[:, :, 1].reshape(384, 192).astype(F32).T.astype(BF)
    for k in (1, 2, 3):
        xk = lax.rem(x + k, 4)
        arrived(w_own.at[xk], r_w.at[10 + xk])
    cp = remote(w_own, w_other, s_w.at[11], r_w.at[14], device(x, y, z, 1 - c))
    cp.start()
    sends.append(cp)

    for k in range(4):
        for d in (2, -2):
            src = ys[k] * 2 + hop(z, d) // 4
            arrived(x_in.at[src], r_x.at[src])
            flat[...] = x_in[src].astype(F32).reshape(640, 128)
            place = pl.ds(pl.multiple_of(src * 48, 16), 48)

            @pl.loop(0, 16)
            def _(r):
                part = flat[pl.ds(r, 40, stride=16), :]
                xt[r, place, :] = jnp.concatenate([part, jnp.zeros((8, 128), F32)], axis=0).astype(BF)

    arrived(mask_in, r_m)

    def sea_rows(r):
        return mask_in[pl.ds(r, 1), :].astype(F32)

    @pl.loop(0, 8)
    def _(i):
        both = jnp.concatenate([xt[2 * i], xt[2 * i + 1]], axis=1)
        stem = jnp.dot(emb_t[...], both, preferred_element_type=F32)
        state[0, 2 * i] = (stem[:, :128] * sea_rows(2 * i)).astype(BF)
        state[0, 2 * i + 1] = (stem[:, 128:] * sea_rows(2 * i + 1)).astype(BF)

    lane = lax.broadcasted_iota(jnp.int32, (16, 128), 1)

    def fold(b):
        for p in range(GROUPS):
            chans = pl.ds(p * 16, 16)

            @pl.when(line == p)
            def _():
                fold_in[b, col_block] = state[b, 13:16, p * 16 : (p + 1) * 16, :]

            @pl.when(line != p)
            def _():
                remote(
                    state.at[b, pl.ds(13, 3), chans, :], fold_in.at[b, col_block],
                    s_f1.at[b, p], r_f1.at[b, col_block], device(x, y, p // 2, p % 2),
                ).start()

        @pl.when(line < GROUPS)
        def _():
            for k in range(1, 16):
                j = lax.rem(col_block + k, 16)
                arrived(fold_in.at[b, j], r_f1.at[b, j])
            rim = jnp.concatenate([fold_in[b, j].reshape(48, 128) for j in range(16)], axis=1)
            column = lax.broadcasted_iota(jnp.int32, (2048, 128), 0)

            @pl.loop(0, 16)
            def _(j):
                onehot = jnp.where(column == partner[pl.ds(j, 1), :], 1.0, 0.0).astype(BF)
                got = jnp.dot(rim, onehot, preferred_element_type=F32).astype(BF)
                for k in range(3):
                    fold_out[b, j, k] = got[(2 - k) * 16 : (3 - k) * 16, :]

            chans = pl.ds(pl.multiple_of(line * 16, 16), 16)
            for j in range(16):
                tj, cj, sj = j // 4, (j // 2) % 2, j % 2
                zj = (tj + 2 + 4 * (sj ^ cj)) % 8

                @pl.when(col_block == j)
                def _():
                    north[b, :, chans, :] = fold_out[b, j]

                @pl.when(col_block != j)
                def _():
                    remote(
                        fold_out.at[b, j], north.at[b, :, chans, :],
                        s_f3.at[b, j], r_f3.at[b, line], device(x, y, zj, cj),
                    ).start()

        for p in range(GROUPS):
            @pl.when(line != p)
            def _():
                arrived(north.at[b, :, pl.ds(p * 16, 16), :], r_f3.at[b, p])

    def fold_sent(b):
        for p in range(GROUPS):
            @pl.when(line != p)
            def _():
                remote(
                    state.at[b, pl.ds(13, 3), pl.ds(p * 16, 16), :], fold_in.at[b, col_block],
                    s_f1.at[b, p], r_f1.at[b, 0], far_dev,
                ).wait_send()

        @pl.when(line < GROUPS)
        def _():
            for j in range(16):
                @pl.when(col_block != j)
                def _():
                    remote(
                        fold_out.at[b, j], fold_out.at[b, j], s_f3.at[b, j], r_f3.at[b, 0], far_dev
                    ).wait_send()

    def halo(b):
        to_north = remote(
            state.at[b, pl.ds(13, 3)], south.at[b], s_halo.at[b, 0], r_halo.at[b, 0], north_dev
        )
        to_south = remote(
            state.at[b, pl.ds(0, 3)], north.at[b], s_halo.at[b, 1], r_halo.at[b, 1], south_dev
        )

        @pl.when(has_north)
        def _():
            to_north.start()

        @pl.when(has_south)
        def _():
            to_south.start()

        @pl.when(on_line)
        def _():
            fold(b)

        @pl.when(has_south)
        def _():
            arrived(south.at[b], r_halo.at[b, 0])

        @pl.when(jnp.logical_not(has_south))
        def _():
            south[b] = jnp.zeros((3, 192, 128), BF)

        @pl.when(has_north)
        def _():
            arrived(north.at[b], r_halo.at[b, 1])

        @pl.loop(0, GROUPS)
        def _(g):
            ch = pl.ds(pl.multiple_of(g * 16, 16), 16)
            to_e = jnp.zeros((16, 128), F32)
            to_w = jnp.zeros((16, 128), F32)
            for r in range(22):
                v = padded_row(b, r, ch)
                here = (lane >= 3 * r) & (lane < 3 * r + 3)
                to_e = jnp.where(here, pltpu.roll(v, (3 * r - 125) % 128, 1), to_e)
                to_w = jnp.where(here, pltpu.roll(v, 3 * r, 1) if r else v, to_w)
            pack_e[b, ch, :] = to_e.astype(BF)
            pack_w[b, ch, :] = to_w.astype(BF)

        go_e = remote(pack_e.at[b], from_w.at[b], s_halo.at[b, 2], r_halo.at[b, 2], east)
        go_w = remote(pack_w.at[b], from_e.at[b], s_halo.at[b, 3], r_halo.at[b, 3], west)
        go_e.start()
        go_w.start()
        sends.append(go_e)
        sends.append(go_w)
        arrived(from_w.at[b], r_halo.at[b, 2])
        arrived(from_e.at[b], r_halo.at[b, 3])
        return to_north, to_south

    def padded_row(b, r, ch):
        if r < 3:
            v = south[b, r, ch, :]
        elif r < 19:
            v = state[b, r - 3, ch, :]
        else:
            v = north[b, r - 19, ch, :]
        return v.astype(F32)

    def depthwise(b):
        @pl.loop(0, GROUPS)
        def _(g):
            ch = pl.ds(pl.multiple_of(g * 16, 16), 16)
            fw = from_w[b, ch, :].astype(F32)
            fe = from_e[b, ch, :].astype(F32)
            for r in range(22):
                xrow[r] = padded_row(b, r, ch)
                left = pltpu.roll(fw, (125 - 3 * r) % 128, 1)
                right = pltpu.roll(fe, (-3 * r) % 128, 1) if r else fe
                srow[r] = jnp.where(lane < 64, right, left)
            taps = dw_all[b, ch, :]
            acc = [None] * 16
            for e in range(7):
                w = [jnp.broadcast_to(taps[:, a * 7 + e : a * 7 + e + 1], (16, 128)) for a in range(7)]
                o = e - 3
                for r in range(22):
                    v = xrow[r]
                    if o < 0:
                        v = pltpu.roll(jnp.where(lane >= 128 + o, srow[r], v), -o, 1)
                    elif o > 0:
                        v = pltpu.roll(jnp.where(lane < o, srow[r], v), 128 - o, 1)
                    for a in range(7):
                        q = r - a
                        if 0 <= q < 16:
                            term = w[a] * v
                            acc[q] = term if acc[q] is None else acc[q] + term
            for q in range(16):
                conv[q, ch, :] = acc[q]

    def pointwise(b):
        down_t[0] = w_own[2 * b + 1].reshape(384, 192).astype(F32).T.astype(BF)
        down_t[1] = w_other[2 * b + 1].reshape(384, 192).astype(F32).T.astype(BF)

        @pl.loop(0, 8)
        def _(i):
            parts = []
            for k in range(2):
                cv = conv[2 * i + k]
                mu = jnp.sum(cv, axis=0, keepdims=True) * (1.0 / 192)
                var = jnp.sum(cv * cv, axis=0, keepdims=True) * (1.0 / 192) - mu * mu
                parts.append(((cv - mu) * lax.rsqrt(var + 1e-6) * gain[b]).astype(BF))
            normed = jnp.concatenate(parts, axis=1)
            branch = jnp.zeros((192, 256), F32)
            for side, w in enumerate((w_own, w_other)):
                pre = jnp.dot(w[2 * b].reshape(384, 192), normed, preferred_element_type=F32)
                hidden = jax.nn.gelu(pre, approximate=True).astype(BF)
                branch = branch + jnp.dot(down_t[side], hidden, preferred_element_type=F32)
            for k in range(2):
                r = 2 * i + k
                new = (state[b, r].astype(F32) + branch[:, k * 128 : (k + 1) * 128]) * sea_rows(r)
                if b == 0:
                    state[1, r] = new.astype(BF)
                else:
                    out_f[pl.ds(r, 192, stride=16), :] = new

    pairs = []
    for b in range(2):
        pairs.append(halo(b))
        depthwise(b)
        if b == 0:
            arrived(w_other, r_w.at[14])
        pointwise(b)

    my_cells = (pl.ds(pl.multiple_of(rb * 16, 16), 16), pl.ds(pl.multiple_of(s * 128, 128), 128))
    for k, yy in enumerate(ys):
        for j, d in enumerate((2, -2)):
            zz = hop(z, d)
            l = yy * 2 + zz // 4
            chans = pl.ds(l * 24, 24)
            out_b[chans] = out_f[pl.ds(pl.multiple_of(l * 384, 384), 384), :].reshape(24, 16, 128).astype(BF)
            cp = remote(
                out_b.at[chans], out.at[:, my_cells[0], my_cells[1]],
                s_o.at[2 * k + j], r_o.at[y * 2 + j], device(x, yy, zz, c),
            )
            cp.start()
            sends.append(cp)
    for k, yy in enumerate(ys):
        for j, d in enumerate((-2, 2)):
            rows, cols = cells_of(yy, hop(z, d))
            arrived(out.at[:, rows, cols], r_o.at[yy * 2 + j])

    w1.wait_send()
    d1.wait_send()
    m_copy.wait_send()
    for cp in sends:
        cp.wait_send()
    for b in range(2):
        to_north, to_south = pairs[b]

        @pl.when(has_north)
        def _():
            to_north.wait_send()

        @pl.when(has_south)
        def _():
            to_south.wait_send()

        @pl.when(on_line)
        def _():
            fold_sent(b)


def body(fields, sea_mask, fold_partner, embed_weight, dw_weight, ln_gain, up_weight, down_weight):
    embed = jnp.pad(embed_weight, ((0, 8), (0, 0)))
    dwg = jnp.concatenate(
        [dw_weight.reshape(2, 24, 49), ln_gain.astype(F32)[:, :, None], jnp.zeros((2, 24, 78), F32)], axis=2
    )
    partner = fold_partner.reshape(16, 128)
    hbm = pl.BlockSpec(memory_space=pl.ANY)
    vmem = pl.BlockSpec(memory_space=pltpu.VMEM)
    dma = pltpu.SemaphoreType.DMA
    scratch = [
        pltpu.VMEM((8, 40, 16, 128), BF),
        pltpu.VMEM((16, 128), jnp.int32),
        pltpu.VMEM((16, 384, 128), BF),
        pltpu.VMEM((640, 128), F32),
        pltpu.VMEM((4, 2, 2, 48, 192), BF),
        pltpu.VMEM((4, 2, 2, 24, 128), F32),
        pltpu.VMEM((2, 192, 128), F32),
        pltpu.VMEM((192, 384), BF),
        pltpu.VMEM((4, 4, 2, 48, 192), BF),
        pltpu.VMEM((4, 4, 2, 48, 192), BF),
        pltpu.VMEM((2, 192, 384), BF),
        pltpu.VMEM((2, 192, 128), F32),
        pltpu.VMEM((16, 192, 128), F32),
        pltpu.VMEM((2, 16, 192, 128), BF),
        pltpu.VMEM((2, 3, 192, 128), BF),
        pltpu.VMEM((2, 3, 192, 128), BF),
        pltpu.VMEM((2, 192, 128), BF),
        pltpu.VMEM((2, 192, 128), BF),
        pltpu.VMEM((2, 192, 128), BF),
        pltpu.VMEM((2, 192, 128), BF),
        pltpu.VMEM((22, 16, 128), F32),
        pltpu.VMEM((22, 16, 128), F32),
        pltpu.VMEM((2, 16, 3, 16, 128), BF),
        pltpu.VMEM((2, 16, 3, 16, 128), BF),
        pltpu.VMEM((192 * 16, 128), F32),
        pltpu.VMEM((192, 16, 128), BF),
        dma((8,)), dma((8,)),
        dma, dma,
        dma((3,)),
        dma((12,)), dma((15,)),
        dma((2, 4)), dma((2, 4)),
        dma((2, 12)), dma((2, 16)),
        dma((2, 16)), dma((2, 12)),
        dma((8,)), dma((8,)),
    ]
    return pl.pallas_call(
        kernel,
        out_shape=jax.ShapeDtypeStruct((24, 64, 256), BF),
        in_specs=[hbm, hbm, vmem, hbm, hbm, hbm, hbm],
        out_specs=hbm,
        scratch_shapes=scratch,
        compiler_params=pltpu.CompilerParams(
            collective_id=0, has_side_effects=True, vmem_limit_bytes=48 * 1024 * 1024
        ),
    )(fields, sea_mask, partner, embed, dwg, up_weight, down_weight)


def solution(mesh):
    in_specs = (
        P("lev", "gy", "gx"),
        P("gy", "gx"),
        P(),
        P("lev", None),
        P(None, "lev", None, None),
        P(None, "lev"),
        P(None, "lev", None),
        P(None, "lev", None),
    )
    out_specs = P("lev", "gy", "gx")
    return jax.shard_map(body, mesh=mesh, in_specs=in_specs, out_specs=out_specs, check_vma=False)
```

```python
import jax
import jax.numpy as jnp
from jax import lax
from jax.experimental import pallas as pl
from jax.experimental.pallas import tpu as pltpu
from jax.sharding import PartitionSpec as P

BF = jnp.bfloat16
F32 = jnp.float32
MESH = pl.DeviceIdType.MESH
GROUPS = 12


def kernel(
    fields, sea, partner, embed, dw_weight, ln_gain, up, down,
    out,
    x_in, sea_in, partner_in, embed_in, dw_raw, gain_raw,
    xt, flat, pe, dw_in, dw_all, emb_t, w_own, w_other, down_t, gain, conv,
    state, south, north, sides, sides_s, sides_n, pack_e, pack_w, from_w, from_e, xrow, srow,
    onehot, fold_in, fold_out, out_f, out_b,
    s_x, r_x, s_loc, s_w, r_w, s_halo, r_halo, s_f1, r_f1, s_f3, r_f3, s_o, r_o,
):
    lev = lax.axis_index("lev")
    x = lax.axis_index("gy")
    gx = lax.axis_index("gx")
    y = lev // 2
    h = lax.rem(lev, 2)
    t = gx // 2
    c = lax.rem(gx, 2)

    def row_block(yy):
        return jnp.where(lax.rem(x, 2) == 0, yy, 3 - yy)

    def half(hh):
        return lax.rem(hh + c, 2)

    def device(xx, yy, hh, tt, cc):
        return (yy * 2 + hh, xx, tt * 2 + cc)

    rb = row_block(y)
    s = half(h)
    col_block = (t * 2 + c) * 2 + s
    line = gx * 2 + h
    on_line = (x == 3) & (rb == 3)
    has_south = jnp.logical_not((x == 0) & (rb == 0))
    has_north = jnp.logical_not(on_line)

    outer_t = lax.rem(t + jnp.where(c == 0, 3, 1), 4)
    far = device(x, y, 1 - h, t, c)
    near = device(x, y, h, jnp.where(h == 0, outer_t, t), 1 - c)
    east_far = h == c
    east = tuple(jnp.where(east_far, f, n) for f, n in zip(far, near))
    west = tuple(jnp.where(east_far, n, f) for f, n in zip(far, near))
    step = jnp.where(lax.rem(x, 2) == 0, 1, -1)
    north_dev = device(
        jnp.where(rb == 3, jnp.minimum(x + 1, 3), x), jnp.where(rb == 3, y, jnp.clip(y + step, 0, 3)), h, t, c
    )
    south_dev = device(
        jnp.where(rb == 0, jnp.maximum(x - 1, 0), x), jnp.where(rb == 0, y, jnp.clip(y - step, 0, 3)), h, t, c
    )

    def remote(src, dst, send, recv, dev):
        return pltpu.make_async_remote_copy(
            src_ref=src, dst_ref=dst, send_sem=send, recv_sem=recv, device_id=dev, device_id_type=MESH
        )

    def arrived(dst, sem):
        remote(dst, dst, s_w.at[0], sem, far).wait_recv()

    ys = [lax.rem(y + k, 4) for k in range(4)]

    def cells_of(yy, hh):
        return (
            pl.ds(pl.multiple_of(row_block(yy) * 16, 16), 16),
            pl.ds(pl.multiple_of(half(hh) * 128, 128), 128),
        )

    my_rows, my_cols = cells_of(y, h)

    half_rows = pl.ds(pl.multiple_of(c * 48, 16), 48)
    slot = pe.at[y, h]
    dslot = dw_in.at[y, h]
    for k, ref in enumerate((up.at[0], down.at[0], up.at[1], down.at[1])):
        @pl.when(x == k)
        def _():
            pltpu.make_async_copy(ref.at[half_rows, :], slot.at[0], s_loc.at[0]).start()
    own = [
        pltpu.make_async_copy(embed, embed_in, s_loc.at[1]),
        pltpu.make_async_copy(dw_weight, dw_raw, s_loc.at[2]),
        pltpu.make_async_copy(ln_gain, gain_raw, s_loc.at[3]),
        pltpu.make_async_copy(sea.at[my_rows, my_cols], sea_in, s_loc.at[4]),
        pltpu.make_async_copy(partner, partner_in, s_loc.at[5]),
        pltpu.make_async_copy(fields.at[:, my_rows, my_cols], x_in.at[lev], s_loc.at[6]),
    ]
    for cp in own:
        cp.start()

    barrier = pltpu.get_barrier_semaphore()
    peers = [device(x, yy, 1 - h, t, c) for yy in ys]
    peers += [device(x, yy, h, t, c) for yy in ys[1:]]
    peers += [device(lax.rem(x + k, 4), y, h, t, c) for k in (1, 2, 3)]
    peers += [device(x, y, h, t, 1 - c)]

    def greet(dev):
        pl.semaphore_signal(barrier, inc=1, device_id=dev, device_id_type=MESH)

    for dev in peers:
        greet(dev)

    @pl.when(on_line)
    def _():
        for k in (1, 2, 3):
            for hh in range(2):
                for cc in range(2):
                    greet(device(x, y, hh, lax.rem(t + k, 4), cc))
        greet(device(x, y, 1 - h, t, 1 - c))

    @pl.when(has_north & (h == 0))
    def _():
        greet(near)

    own[0].wait()
    own[1].wait()
    own[2].wait()
    slot[1] = jnp.concatenate([embed_in[...].astype(F32), jnp.zeros((8, 192), F32)], axis=0).astype(BF)
    diagonal = lax.broadcasted_iota(jnp.int32, (24, 24), 0) == lax.broadcasted_iota(jnp.int32, (24, 24), 1)
    gains = gain_raw[...].astype(F32)
    for b in range(2):
        raw = dw_raw[b]
        column = jnp.sum(jnp.where(diagonal, gains[b : b + 1, :], 0.0), axis=1, keepdims=True)
        dslot[b] = jnp.concatenate(
            [raw[:, a, :] for a in range(7)] + [column, jnp.zeros((24, 78), F32)], axis=1
        )
    pltpu.make_async_copy(up.at[0].at[half_rows, :], slot.at[0], s_loc.at[0]).wait()

    pl.semaphore_wait(barrier, len(peers) + jnp.where(on_line, 13, 1 - h))

    sends = []

    def send(src, dst, send_sem, recv_sem, dev):
        cp = remote(src, dst, send_sem, recv_sem, dev)
        cp.start()
        sends.append(cp)

    send(slot, slot, s_w.at[0], r_w.at[0], far)
    send(dslot, dslot, s_w.at[1], r_w.at[1], far)

    others = [(k, 1) for k in range(4)] + [(k, 0) for k in range(1, 4)]
    for i, (k, flip) in enumerate(others):
        hh = lax.rem(h + flip, 2)
        rows, cols = cells_of(ys[k], hh)
        send(
            fields.at[:, rows, cols], x_in.at[lev], s_x.at[i], r_x.at[lev], device(x, ys[k], hh, t, c)
        )

    arrived(pe.at[y, 1 - h], r_w.at[0])
    arrived(dw_in.at[y, 1 - h], r_w.at[1])
    for k in (1, 2, 3):
        dev = device(x, ys[k], h, t, c)
        send(pe.at[y], pe.at[y], s_w.at[2 * k], r_w.at[2 + y], dev)
        send(dw_in.at[y], dw_in.at[y], s_w.at[2 * k + 1], r_w.at[6 + y], dev)

    own[4].wait()

    @pl.when(on_line & (line < GROUPS))
    def _():
        @pl.loop(0, 8)
        def _(j):
            @pl.loop(0, 16)
            def _(m):
                source = lax.broadcasted_iota(jnp.int32, (128, 128), 0) + m * 128
                for q in range(2):
                    hit = source == partner_in[pl.ds(2 * j + q, 1), :]
                    onehot[j, pl.ds(pl.multiple_of(m * 128, 128), 128), q * 128 : (q + 1) * 128] = jnp.where(
                        hit, 1.0, 0.0
                    ).astype(BF)

    for k in (1, 2, 3):
        arrived(pe.at[ys[k]], r_w.at[2 + ys[k]])
        arrived(dw_in.at[ys[k]], r_w.at[6 + ys[k]])

    for k in (1, 2, 3):
        send(
            pe.at[:, :, 0], w_own.at[x], s_w.at[7 + k], r_w.at[10 + x], device(lax.rem(x + k, 4), y, h, t, c)
        )
    w_own[x] = pe[:, :, 0]
    for l in range(8):
        for b in range(2):
            dw_all[b, l * 24 : (l + 1) * 24, :] = dw_in[l // 2, l % 2, b]
    for b in range(2):
        gain[b] = jnp.broadcast_to(dw_all[b, :, 49:50], (192, 128))
    emb_t[...] = pe[:, :, 1].reshape(384, 192).astype(F32).T.astype(BF)
    for k in (1, 2, 3):
        xk = lax.rem(x + k, 4)
        arrived(w_own.at[xk], r_w.at[10 + xk])
    send(w_own, w_other, s_w.at[11], r_w.at[14], device(x, y, h, t, 1 - c))

    own[5].wait()
    for k, flip in [(0, 0)] + others[4:] + others[:4]:
        src = ys[k] * 2 + lax.rem(h + flip, 2)
        if (k, flip) != (0, 0):
            arrived(x_in.at[src], r_x.at[src])
        flat[...] = x_in[src].astype(F32).reshape(640, 128)
        place = pl.ds(pl.multiple_of(src * 48, 16), 48)

        @pl.loop(0, 16)
        def _(r):
            part = flat[pl.ds(r, 40, stride=16), :]
            xt[r, place, :] = jnp.concatenate([part, jnp.zeros((8, 128), F32)], axis=0).astype(BF)

    own[3].wait()

    def sea_rows(r):
        return sea_in[pl.ds(r, 1), :].astype(F32)

    @pl.loop(0, 4)
    def _(n):
        for q in range(2):
            r = 4 * n + 2 * q
            both = jnp.concatenate([xt[r], xt[r + 1]], axis=1)
            stem = jnp.dot(emb_t[...], both, preferred_element_type=F32)
            state[0, r] = (stem[:, :128] * sea_rows(r)).astype(BF)
            state[0, r + 1] = (stem[:, 128:] * sea_rows(r + 1)).astype(BF)

    lane = lax.broadcasted_iota(jnp.int32, (16, 128), 1)

    def group(g):
        return pl.ds(pl.multiple_of(g * 16, 16), 16)

    def rim_copy(b, p):
        return remote(
            state.at[b, pl.ds(13, 3), pl.ds(p * 16, 16), :], fold_in.at[b, col_block],
            s_f1.at[b, p], r_f1.at[b, col_block], device(x, y, p % 2, p // 4, (p // 2) % 2),
        )

    def ghost_copy(b, j):
        tj, cj, sj = j // 4, (j // 2) % 2, j % 2
        return remote(
            fold_out.at[b, j], north.at[b, :, :, group(line), :],
            s_f3.at[b, j], r_f3.at[b, line], device(x, y, sj ^ cj, tj, cj),
        )

    def row_copies(b):
        return (
            remote(state.at[b, pl.ds(13, 3)], south.at[b], s_halo.at[b, 0], r_halo.at[b, 0], north_dev),
            remote(state.at[b, pl.ds(0, 3)], north.at[b, 0], s_halo.at[b, 1], r_halo.at[b, 1], south_dev),
        )

    def side_copies(b):
        return (
            remote(sides.at[b], sides_s.at[b], s_halo.at[b, 4], r_halo.at[b, 4], north_dev),
            remote(sides.at[b], sides_n.at[b], s_halo.at[b, 5], r_halo.at[b, 5], south_dev),
        )

    def start_pair(pair):
        @pl.when(has_north)
        def _():
            pair[0].start()

        @pl.when(has_south)
        def _():
            pair[1].start()

    def halo_start(b):
        @pl.when(on_line)
        def _():
            for p in range(GROUPS):
                @pl.when(line == p)
                def _():
                    fold_in[b, col_block] = state[b, 13:16, p * 16 : (p + 1) * 16, :]

                @pl.when(line != p)
                def _():
                    rim_copy(b, p).start()

        start_pair(row_copies(b))

        @pl.loop(0, GROUPS)
        def _(g):
            ch = group(g)
            to_e = jnp.zeros((16, 128), F32)
            to_w = jnp.zeros((16, 128), F32)
            for r in range(16):
                v = state[b, r, ch, :].astype(F32)
                xrow[r + 3, ch, :] = v
                to_e = jnp.where(
                    (lane >= 3 * r) & (lane < 3 * r + 3), pltpu.roll(v, (3 * r - 125) % 128, 1), to_e
                )
                to_w = jnp.where(
                    (lane >= 64 + 3 * r) & (lane < 67 + 3 * r), pltpu.roll(v, 64 + 3 * r, 1), to_w
                )
            pack_e[b, ch, :] = to_e.astype(BF)
            pack_w[b, ch, :] = to_w.astype(BF)

        send(pack_e.at[b], from_w.at[b], s_halo.at[b, 2], r_halo.at[b, 2], east)
        send(pack_w.at[b], from_e.at[b], s_halo.at[b, 3], r_halo.at[b, 3], west)

    def fold(b):
        for k in range(1, 16):
            j = lax.rem(col_block + k, 16)
            arrived(fold_in.at[b, j], r_f1.at[b, j])
        rim = jnp.concatenate([fold_in[b, j].reshape(48, 128) for j in range(16)], axis=1)

        @pl.loop(0, 8)
        def _(j):
            got = jnp.dot(rim, onehot[j], preferred_element_type=F32).astype(BF)
            for q in range(2):
                for k in range(3):
                    fold_out[b, 2 * j + q, 0, k] = got[(2 - k) * 16 : (3 - k) * 16, q * 128 : (q + 1) * 128]

        @pl.loop(0, 16)
        def _(j):
            for k in range(3):
                after = fold_out[b, lax.rem(j + 1, 16), 0, k].astype(F32)
                before = fold_out[b, lax.rem(j + 15, 16), 0, k].astype(F32)
                fold_out[b, j, 1, k] = jnp.where(lane < 64, after, before).astype(BF)

        for j in range(16):
            @pl.when(col_block == j)
            def _():
                north[b, :, :, group(line), :] = fold_out[b, j]

            @pl.when(col_block != j)
            def _():
                ghost_copy(b, j).start()

    def halo_middle(b):
        @pl.when(on_line & (line < GROUPS))
        def _():
            fold(b)

        arrived(from_w.at[b], r_halo.at[b, 2])
        arrived(from_e.at[b], r_halo.at[b, 3])
        west_lanes = lax.broadcasted_iota(jnp.int32, (192, 128), 1) < 64
        sides[b] = jnp.where(west_lanes, from_w[b].astype(F32), from_e[b].astype(F32)).astype(BF)
        start_pair(side_copies(b))

    def halo_end(b):
        @pl.when(has_south)
        def _():
            arrived(south.at[b], r_halo.at[b, 0])
            arrived(sides_s.at[b], r_halo.at[b, 4])

        @pl.when(jnp.logical_not(has_south))
        def _():
            south[b] = jnp.zeros((3, 192, 128), BF)
            sides_s[b] = jnp.zeros((192, 128), BF)

        @pl.when(has_north)
        def _():
            arrived(north.at[b, 0], r_halo.at[b, 1])
            arrived(sides_n.at[b], r_halo.at[b, 5])

        @pl.when(on_line)
        def _():
            for p in range(GROUPS):
                @pl.when(line != p)
                def _():
                    arrived(north.at[b, :, :, pl.ds(p * 16, 16), :], r_f3.at[b, p])

    def halo_sent(b):
        for pair in (row_copies(b), side_copies(b)):
            @pl.when(has_north)
            def _():
                pair[0].wait_send()

            @pl.when(has_south)
            def _():
                pair[1].wait_send()

        @pl.when(on_line)
        def _():
            for p in range(GROUPS):
                @pl.when(line != p)
                def _():
                    rim_copy(b, p).wait_send()

            @pl.when(line < GROUPS)
            def _():
                for j in range(16):
                    @pl.when(col_block != j)
                    def _():
                        ghost_copy(b, j).wait_send()

    def side_tile(tile, r):
        left = pltpu.roll(tile, (125 - 3 * r) % 128, 1)
        right = pltpu.roll(tile, (64 - 3 * r) % 128, 1)
        return jnp.where(lane < 64, right, left)

    def depthwise(b, inner):
        spans = ((3, 13),) if inner else ((0, 3), (13, 16))

        @pl.loop(0, GROUPS)
        def _(g):
            ch = group(g)
            if inner:
                tile = sides[b, ch, :].astype(F32)
                for r in range(16):
                    srow[r + 3, ch, :] = side_tile(tile, r)
            else:
                tile = sides_s[b, ch, :].astype(F32)
                for r in range(3):
                    xrow[r, ch, :] = south[b, r, ch, :].astype(F32)
                    srow[r, ch, :] = side_tile(tile, r + 13)
                    xrow[r + 19, ch, :] = north[b, 0, r, ch, :].astype(F32)

                @pl.when(has_north)
                def _():
                    tile = sides_n[b, ch, :].astype(F32)
                    for r in range(3):
                        srow[r + 19, ch, :] = side_tile(tile, r)

                @pl.when(on_line)
                def _():
                    for r in range(3):
                        srow[r + 19, ch, :] = north[b, 1, r, ch, :].astype(F32)

            taps = dw_all[b, ch, :]
            acc = [None] * 16
            for e in range(7):
                w = [jnp.broadcast_to(taps[:, a * 7 + e : a * 7 + e + 1], (16, 128)) for a in range(7)]
                o = e - 3
                for lo, hi in spans:
                    for r in range(lo, hi + 6):
                        v = xrow[r, ch, :]
                        if o < 0:
                            v = pltpu.roll(jnp.where(lane >= 128 + o, srow[r, ch, :], v), -o, 1)
                        elif o > 0:
                            v = pltpu.roll(jnp.where(lane < o, srow[r, ch, :], v), 128 - o, 1)
                        for a in range(7):
                            q = r - a
                            if lo <= q < hi:
                                term = w[a] * v
                                acc[q] = term if acc[q] is None else acc[q] + term
            for lo, hi in spans:
                for q in range(lo, hi):
                    conv[q, ch, :] = acc[q]

    def pointwise(b, first):
        @pl.loop(0, 2)
        def _(n):
            for q in range(2):
                i = first(n) + q
                parts = []
                for k in range(2):
                    cv = conv[2 * i + k]
                    mu = jnp.sum(cv, axis=0, keepdims=True) * (1.0 / 192)
                    var = jnp.sum(cv * cv, axis=0, keepdims=True) * (1.0 / 192) - mu * mu
                    parts.append(((cv - mu) * lax.rsqrt(var + 1e-6) * gain[b]).astype(BF))
                normed = jnp.concatenate(parts, axis=1)
                branch = jnp.zeros((192, 256), F32)
                for side, w in enumerate((w_own, w_other)):
                    pre = jnp.dot(w[2 * b].reshape(384, 192), normed, preferred_element_type=F32)
                    hidden = jax.nn.gelu(pre, approximate=True).astype(BF)
                    branch = branch + jnp.dot(down_t[b, side], hidden, preferred_element_type=F32)
                for k in range(2):
                    r = 2 * i + k
                    new = (state[b, r].astype(F32) + branch[:, k * 128 : (k + 1) * 128]) * sea_rows(r)
                    if b == 0:
                        state[1, r] = new.astype(BF)
                    else:
                        out_f[pl.ds(r, 192, stride=16), :] = new

    for b in range(2):
        halo_start(b)
        if b == 0:
            arrived(w_other, r_w.at[14])
            for bb in range(2):
                for side, w in enumerate((w_own, w_other)):
                    down_t[bb, side] = w[2 * bb + 1].reshape(384, 192).astype(F32).T.astype(BF)
        halo_middle(b)
        depthwise(b, True)
        pointwise(b, lambda n: 2 + 2 * n)
        halo_end(b)
        depthwise(b, False)
        pointwise(b, lambda n: 6 * n)

    def chunk(l):
        chans = pl.ds(l * 24, 24)
        out_b[chans] = out_f[pl.ds(pl.multiple_of(l * 384, 384), 384), :].reshape(24, 16, 128).astype(BF)
        return out_b.at[chans]

    for i, (k, flip) in enumerate(others):
        hh = lax.rem(h + flip, 2)
        send(
            chunk(ys[k] * 2 + hh), out.at[:, my_rows, my_cols], s_o.at[i], r_o.at[lev], device(x, ys[k], hh, t, c)
        )
    last = pltpu.make_async_copy(chunk(lev), out.at[:, my_rows, my_cols], s_o.at[7])
    last.start()
    for k, flip in others:
        hh = lax.rem(h + flip, 2)
        rows, cols = cells_of(ys[k], hh)
        arrived(out.at[:, rows, cols], r_o.at[ys[k] * 2 + hh])
    last.wait()
    for cp in sends:
        cp.wait_send()
    for b in range(2):
        halo_sent(b)


def body(fields, sea_mask, fold_partner, embed_weight, dw_weight, ln_gain, up_weight, down_weight):
    partner = fold_partner.reshape(16, 128)
    hbm = pl.BlockSpec(memory_space=pl.ANY)
    dma = pltpu.SemaphoreType.DMA
    scratch = [
        pltpu.VMEM((8, 40, 16, 128), BF),
        pltpu.VMEM((16, 128), jnp.int32),
        pltpu.VMEM((16, 128), jnp.int32),
        pltpu.VMEM((40, 192), BF),
        pltpu.VMEM((2, 24, 7, 7), F32),
        pltpu.VMEM((2, 24), BF),
        pltpu.VMEM((16, 384, 128), BF),
        pltpu.VMEM((640, 128), F32),
        pltpu.VMEM((4, 2, 2, 48, 192), BF),
        pltpu.VMEM((4, 2, 2, 24, 128), F32),
        pltpu.VMEM((2, 192, 128), F32),
        pltpu.VMEM((192, 384), BF),
        pltpu.VMEM((4, 4, 2, 48, 192), BF),
        pltpu.VMEM((4, 4, 2, 48, 192), BF),
        pltpu.VMEM((2, 2, 192, 384), BF),
        pltpu.VMEM((2, 192, 128), F32),
        pltpu.VMEM((16, 192, 128), F32),
        pltpu.VMEM((2, 16, 192, 128), BF),
        pltpu.VMEM((2, 3, 192, 128), BF),
        pltpu.VMEM((2, 2, 3, 192, 128), BF),
        pltpu.VMEM((2, 192, 128), BF),
        pltpu.VMEM((2, 192, 128), BF),
        pltpu.VMEM((2, 192, 128), BF),
        pltpu.VMEM((2, 192, 128), BF),
        pltpu.VMEM((2, 192, 128), BF),
        pltpu.VMEM((2, 192, 128), BF),
        pltpu.VMEM((2, 192, 128), BF),
        pltpu.VMEM((22, 192, 128), F32),
        pltpu.VMEM((22, 192, 128), F32),
        pltpu.VMEM((8, 2048, 256), BF),
        pltpu.VMEM((2, 16, 3, 16, 128), BF),
        pltpu.VMEM((2, 16, 2, 3, 16, 128), BF),
        pltpu.VMEM((192 * 16, 128), F32),
        pltpu.VMEM((192, 16, 128), BF),
        dma((7,)), dma((8,)),
        dma((7,)),
        dma((12,)), dma((15,)),
        dma((2, 6)), dma((2, 6)),
        dma((2, 12)), dma((2, 16)),
        dma((2, 16)), dma((2, 12)),
        dma((8,)), dma((8,)),
    ]
    return pl.pallas_call(
        kernel,
        out_shape=jax.ShapeDtypeStruct((24, 64, 256), BF),
        in_specs=[hbm] * 8,
        out_specs=hbm,
        scratch_shapes=scratch,
        compiler_params=pltpu.CompilerParams(
            collective_id=0, has_side_effects=True, vmem_limit_bytes=60 * 1024 * 1024
        ),
    )(fields, sea_mask, partner, embed_weight, dw_weight, ln_gain, up_weight, down_weight)


def solution(mesh):
    in_specs = (
        P("lev", "gy", "gx"),
        P("gy", "gx"),
        P(),
        P("lev", None),
        P(None, "lev", None, None),
        P(None, "lev"),
        P(None, "lev", None),
        P(None, "lev", None),
    )
    out_specs = P("lev", "gy", "gx")
    return jax.shard_map(body, mesh=mesh, in_specs=in_specs, out_specs=out_specs, check_vma=False)
```

```python
import jax
import jax.numpy as jnp
from jax import lax
from jax.experimental import pallas as pl
from jax.experimental.pallas import tpu as pltpu
from jax.sharding import PartitionSpec as P

BF = jnp.bfloat16
F32 = jnp.float32
MESH = pl.DeviceIdType.MESH
GROUPS = 12


def twice_gelu(v):
    inner = v * (0.7978845608028654 + 0.035677408136300125 * (v * v))
    return v + v * jnp.tanh(inner)


def kernel(
    fields, sea, partner, embed, dw_weight, ln_gain, up, down,
    out,
    x_in, sea_in, partner_in, embed_in, dw_raw, gain_raw,
    xt, flat, pe, dw_in, dw_all, taps, end_taps, emb_t, w_own, w_other, down_t, gain, conv,
    state, south, north, diff, diff_s, diff_n, pack, from_w, from_e, xrow,
    onehot, fold_in, fold_out, out_f, out_b,
    s_x, r_x, s_loc, s_w, r_w, s_halo, r_halo, s_f1, r_f1, s_f3, r_f3, s_o, r_o,
):
    lev = lax.axis_index("lev")
    x = lax.axis_index("gy")
    gx = lax.axis_index("gx")
    y = lev // 2
    h = lax.rem(lev, 2)
    t = gx // 2
    c = lax.rem(gx, 2)

    def row_block(yy):
        return jnp.where(lax.rem(x, 2) == 0, yy, 3 - yy)

    def half(hh):
        return lax.rem(hh + c, 2)

    def device(xx, yy, hh, tt, cc):
        return (yy * 2 + hh, xx, tt * 2 + cc)

    rb = row_block(y)
    s = half(h)
    col_block = (t * 2 + c) * 2 + s
    line = gx * 2 + h
    on_line = (x == 3) & (rb == 3)
    has_south = jnp.logical_not((x == 0) & (rb == 0))
    has_north = jnp.logical_not(on_line)

    outer_t = lax.rem(t + jnp.where(c == 0, 3, 1), 4)
    far = device(x, y, 1 - h, t, c)
    near = device(x, y, h, jnp.where(h == 0, outer_t, t), 1 - c)
    east_far = h == c
    east = tuple(jnp.where(east_far, f, n) for f, n in zip(far, near))
    west = tuple(jnp.where(east_far, n, f) for f, n in zip(far, near))
    step = jnp.where(lax.rem(x, 2) == 0, 1, -1)
    north_dev = device(
        jnp.where(rb == 3, jnp.minimum(x + 1, 3), x), jnp.where(rb == 3, y, jnp.clip(y + step, 0, 3)), h, t, c
    )
    south_dev = device(
        jnp.where(rb == 0, jnp.maximum(x - 1, 0), x), jnp.where(rb == 0, y, jnp.clip(y - step, 0, 3)), h, t, c
    )

    def remote(src, dst, send, recv, dev):
        return pltpu.make_async_remote_copy(
            src_ref=src, dst_ref=dst, send_sem=send, recv_sem=recv, device_id=dev, device_id_type=MESH
        )

    def arrived(dst, sem):
        remote(dst, dst, s_w.at[0], sem, far).wait_recv()

    ys = [lax.rem(y + k, 4) for k in range(4)]

    def cells_of(yy, hh):
        return (
            pl.ds(pl.multiple_of(row_block(yy) * 16, 16), 16),
            pl.ds(pl.multiple_of(half(hh) * 128, 128), 128),
        )

    my_rows, my_cols = cells_of(y, h)

    half_rows = pl.ds(pl.multiple_of(c * 48, 16), 48)
    slot = pe.at[y, h]
    dslot = dw_in.at[y, h]
    for k, ref in enumerate((up.at[0], down.at[0], up.at[1], down.at[1])):
        @pl.when(x == k)
        def _():
            pltpu.make_async_copy(ref.at[half_rows, :], slot.at[0], s_loc.at[0]).start()
    own = [
        pltpu.make_async_copy(embed, embed_in, s_loc.at[1]),
        pltpu.make_async_copy(dw_weight, dw_raw, s_loc.at[2]),
        pltpu.make_async_copy(ln_gain, gain_raw, s_loc.at[3]),
        pltpu.make_async_copy(sea.at[my_rows, my_cols], sea_in, s_loc.at[4]),
        pltpu.make_async_copy(partner, partner_in, s_loc.at[5]),
        pltpu.make_async_copy(fields.at[:, my_rows, my_cols], x_in.at[lev], s_loc.at[6]),
    ]
    for cp in own:
        cp.start()

    barrier = pltpu.get_barrier_semaphore()
    peers = [device(x, yy, 1 - h, t, c) for yy in ys]
    peers += [device(x, yy, h, t, c) for yy in ys[1:]]
    peers += [device(lax.rem(x + k, 4), y, h, t, c) for k in (1, 2, 3)]
    peers += [device(x, y, h, t, 1 - c)]

    def greet(dev):
        pl.semaphore_signal(barrier, inc=1, device_id=dev, device_id_type=MESH)

    for dev in peers:
        greet(dev)

    @pl.when(on_line)
    def _():
        for k in (1, 2, 3):
            for hh in range(2):
                for cc in range(2):
                    greet(device(x, y, hh, lax.rem(t + k, 4), cc))
        greet(device(x, y, 1 - h, t, 1 - c))

    @pl.when(has_north & (h == 0))
    def _():
        greet(near)

    own[0].wait()
    own[1].wait()
    own[2].wait()
    slot[1] = jnp.concatenate([embed_in[...].astype(F32), jnp.zeros((8, 192), F32)], axis=0).astype(BF)
    diagonal = lax.broadcasted_iota(jnp.int32, (24, 24), 0) == lax.broadcasted_iota(jnp.int32, (24, 24), 1)
    gains = gain_raw[...].astype(F32)
    for b in range(2):
        raw = dw_raw[b]
        column = jnp.sum(jnp.where(diagonal, gains[b : b + 1, :], 0.0), axis=1, keepdims=True)
        dslot[b] = jnp.concatenate(
            [raw[:, a, :] for a in range(7)] + [column, jnp.zeros((24, 78), F32)], axis=1
        )
    pltpu.make_async_copy(up.at[0].at[half_rows, :], slot.at[0], s_loc.at[0]).wait()

    pl.semaphore_wait(barrier, len(peers) + jnp.where(on_line, 13, 1 - h))

    sends = []

    def send(src, dst, send_sem, recv_sem, dev):
        cp = remote(src, dst, send_sem, recv_sem, dev)
        cp.start()
        sends.append(cp)

    send(slot, slot, s_w.at[0], r_w.at[0], far)
    send(dslot, dslot, s_w.at[1], r_w.at[1], far)

    others = [(k, 1) for k in range(4)] + [(k, 0) for k in range(1, 4)]
    for i, (k, flip) in enumerate(others):
        hh = lax.rem(h + flip, 2)
        rows, cols = cells_of(ys[k], hh)
        send(
            fields.at[:, rows, cols], x_in.at[lev], s_x.at[i], r_x.at[lev], device(x, ys[k], hh, t, c)
        )

    arrived(pe.at[y, 1 - h], r_w.at[0])
    arrived(dw_in.at[y, 1 - h], r_w.at[1])
    for k in (1, 2, 3):
        dev = device(x, ys[k], h, t, c)
        send(pe.at[y], pe.at[y], s_w.at[2 * k], r_w.at[2 + y], dev)
        send(dw_in.at[y], dw_in.at[y], s_w.at[2 * k + 1], r_w.at[6 + y], dev)

    own[4].wait()

    @pl.when(on_line & (line < GROUPS))
    def _():
        @pl.loop(0, 8)
        def _(j):
            @pl.loop(0, 16)
            def _(m):
                source = lax.broadcasted_iota(jnp.int32, (128, 128), 0) + m * 128
                for q in range(2):
                    hit = source == partner_in[pl.ds(2 * j + q, 1), :]
                    onehot[j, pl.ds(pl.multiple_of(m * 128, 128), 128), q * 128 : (q + 1) * 128] = jnp.where(
                        hit, 1.0, 0.0
                    ).astype(BF)

    for k in (1, 2, 3):
        arrived(pe.at[ys[k]], r_w.at[2 + ys[k]])
        arrived(dw_in.at[ys[k]], r_w.at[6 + ys[k]])

    for k in (1, 2, 3):
        send(
            pe.at[:, :, 0], w_own.at[x], s_w.at[7 + k], r_w.at[10 + x], device(lax.rem(x + k, 4), y, h, t, c)
        )
    w_own[x] = pe[:, :, 0]
    for l in range(8):
        for b in range(2):
            dw_all[b, l * 24 : (l + 1) * 24, :] = dw_in[l // 2, l % 2, b]
    for b in range(2):
        gain[b] = jnp.broadcast_to(dw_all[b, :, 49:50], (192, 128))
    west16 = lax.rem(lax.broadcasted_iota(jnp.int32, (16, 128), 1), 6) >= 3
    for b in range(2):
        @pl.loop(0, GROUPS)
        def _(g):
            ch = pl.ds(pl.multiple_of(g * 16, 16), 16)
            row = dw_all[b, ch, :]
            wide = [jnp.broadcast_to(row[:, k : k + 1], (16, 128)) for k in range(49)]
            for k in range(49):
                taps[b, k, ch, :] = wide[k]
            for a in range(7):
                for d in range(3):
                    end_taps[b, a * 3 + d, ch, :] = jnp.where(west16, wide[a * 7 + d], wide[a * 7 + 4 + d])

    emb_t[...] = pe[:, :, 1].reshape(384, 192).astype(F32).T.astype(BF)
    for k in (1, 2, 3):
        xk = lax.rem(x + k, 4)
        arrived(w_own.at[xk], r_w.at[10 + xk])
    send(w_own, w_other, s_w.at[11], r_w.at[14], device(x, y, h, t, 1 - c))

    own[5].wait()
    for k, flip in [(0, 0)] + others[4:] + others[:4]:
        src = ys[k] * 2 + lax.rem(h + flip, 2)
        if (k, flip) != (0, 0):
            arrived(x_in.at[src], r_x.at[src])
        flat[...] = x_in[src].astype(F32).reshape(640, 128)
        place = pl.ds(pl.multiple_of(src * 48, 16), 48)

        @pl.loop(0, 16)
        def _(r):
            part = flat[pl.ds(r, 40, stride=16), :]
            xt[r, place, :] = jnp.concatenate([part, jnp.zeros((8, 128), F32)], axis=0).astype(BF)

    own[3].wait()

    def sea_rows(r):
        return sea_in[pl.ds(r, 1), :].astype(F32)

    @pl.loop(0, 4)
    def _(n):
        for q in range(2):
            r = 4 * n + 2 * q
            both = jnp.concatenate([xt[r], xt[r + 1]], axis=1)
            stem = jnp.dot(emb_t[...], both, preferred_element_type=F32)
            state[0, r] = (stem[:, :128] * sea_rows(r)).astype(BF)
            state[0, r + 1] = (stem[:, 128:] * sea_rows(r + 1)).astype(BF)

    lane = lax.broadcasted_iota(jnp.int32, (16, 128), 1)

    wide_lane = lax.broadcasted_iota(jnp.int32, (192, 128), 1)
    west_slot = lax.rem(wide_lane, 6) >= 3
    place = lax.rem(wide_lane, 3)
    row_ends = (wide_lane < 3) | (wide_lane >= 125)

    def group(g):
        return pl.ds(pl.multiple_of(g * 16, 16), 16)

    def rim_copy(b, p):
        return remote(
            state.at[b, pl.ds(13, 3), pl.ds(p * 16, 16), :], fold_in.at[b, col_block],
            s_f1.at[b, p], r_f1.at[b, col_block], device(x, y, p % 2, p // 4, (p // 2) % 2),
        )

    def ghost_copy(b, j):
        tj, cj, sj = j // 4, (j // 2) % 2, j % 2
        return remote(
            fold_out.at[b, j], north.at[b, :, :, group(line), :],
            s_f3.at[b, j], r_f3.at[b, line], device(x, y, sj ^ cj, tj, cj),
        )

    def row_copies(b):
        return (
            remote(state.at[b, pl.ds(13, 3)], south.at[b], s_halo.at[b, 0], r_halo.at[b, 0], north_dev),
            remote(state.at[b, pl.ds(0, 3)], north.at[b, 0], s_halo.at[b, 1], r_halo.at[b, 1], south_dev),
        )

    def side_copies(b):
        return (
            remote(diff.at[b], diff_s.at[b], s_halo.at[b, 4], r_halo.at[b, 4], north_dev),
            remote(diff.at[b], diff_n.at[b], s_halo.at[b, 5], r_halo.at[b, 5], south_dev),
        )

    def start_pair(pair):
        @pl.when(has_north)
        def _():
            pair[0].start()

        @pl.when(has_south)
        def _():
            pair[1].start()

    def halo_start(b):
        @pl.when(on_line)
        def _():
            for p in range(GROUPS):
                @pl.when(line == p)
                def _():
                    fold_in[b, col_block] = state[b, 13:16, p * 16 : (p + 1) * 16, :]

                @pl.when(line != p)
                def _():
                    rim_copy(b, p).start()

        start_pair(row_copies(b))

        @pl.loop(0, 2)
        def _(g):
            ch = pl.ds(pl.multiple_of(g * 96, 96), 96)
            lane96 = lax.broadcasted_iota(jnp.int32, (96, 128), 1)
            tile = jnp.zeros((96, 128), F32)
            for r in range(16):
                v = state[b, r, ch, :].astype(F32)
                xrow[r + 3, ch, :] = v
                tile = jnp.where((lane96 >= 6 * r) & (lane96 < 6 * r + 6), pltpu.roll(v, 6 * r + 3, 1), tile)
            pack[b, ch, :] = tile.astype(BF)

        send(pack.at[b], from_w.at[b], s_halo.at[b, 2], r_halo.at[b, 2], east)
        send(pack.at[b], from_e.at[b], s_halo.at[b, 3], r_halo.at[b, 3], west)

    def fold(b):
        for k in range(1, 16):
            j = lax.rem(col_block + k, 16)
            arrived(fold_in.at[b, j], r_f1.at[b, j])
        rim = jnp.concatenate([fold_in[b, j].reshape(48, 128) for j in range(16)], axis=1)

        @pl.loop(0, 8)
        def _(j):
            got = jnp.dot(rim, onehot[j], preferred_element_type=F32).astype(BF)
            for q in range(2):
                for k in range(3):
                    fold_out[b, 2 * j + q, 0, k] = got[(2 - k) * 16 : (3 - k) * 16, q * 128 : (q + 1) * 128]

        @pl.loop(0, 16)
        def _(j):
            for k in range(3):
                after = fold_out[b, lax.rem(j + 1, 16), 0, k].astype(F32)
                before = fold_out[b, lax.rem(j + 15, 16), 0, k].astype(F32)
                fold_out[b, j, 1, k] = jnp.where(lane < 64, after, before).astype(BF)

        for j in range(16):
            @pl.when(col_block == j)
            def _():
                north[b, :, :, group(line), :] = fold_out[b, j]

            @pl.when(col_block != j)
            def _():
                ghost_copy(b, j).start()

    def halo_middle(b):
        @pl.when(on_line & (line < GROUPS))
        def _():
            fold(b)

        arrived(from_w.at[b], r_halo.at[b, 2])
        arrived(from_e.at[b], r_halo.at[b, 3])
        mine = pack[b].astype(F32)
        diff[b] = jnp.where(
            west_slot,
            pltpu.roll(from_w[b].astype(F32) - mine, 3, 1),
            pltpu.roll(from_e[b].astype(F32) - mine, 125, 1),
        )
        start_pair(side_copies(b))

    def halo_end(b):
        @pl.when(has_south)
        def _():
            arrived(south.at[b], r_halo.at[b, 0])
            arrived(diff_s.at[b], r_halo.at[b, 4])

        @pl.when(jnp.logical_not(has_south))
        def _():
            south[b] = jnp.zeros((3, 192, 128), BF)
            diff_s[b] = jnp.zeros((192, 128), F32)

        @pl.when(has_north)
        def _():
            arrived(north.at[b, 0], r_halo.at[b, 1])
            arrived(diff_n.at[b], r_halo.at[b, 5])

        @pl.when(on_line)
        def _():
            for p in range(GROUPS):
                @pl.when(line != p)
                def _():
                    arrived(north.at[b, :, :, pl.ds(p * 16, 16), :], r_f3.at[b, p])

            @pl.loop(0, GROUPS)
            def _(g):
                ch = group(g)
                tile = jnp.zeros((16, 128), F32)
                for r in range(3):
                    d = north[b, 1, r, ch, :].astype(F32) - north[b, 0, r, ch, :].astype(F32)
                    tile = jnp.where((lane >= 6 * r) & (lane < 6 * r + 3), pltpu.roll(d, 6 * r, 1), tile)
                    tile = jnp.where(
                        (lane >= 6 * r + 3) & (lane < 6 * r + 6), pltpu.roll(d, 6 * r + 6, 1), tile
                    )
                diff_n[b, ch, :] = tile

    def halo_sent(b):
        for pair in (row_copies(b), side_copies(b)):
            @pl.when(has_north)
            def _():
                pair[0].wait_send()

            @pl.when(has_south)
            def _():
                pair[1].wait_send()

        @pl.when(on_line)
        def _():
            for p in range(GROUPS):
                @pl.when(line != p)
                def _():
                    rim_copy(b, p).wait_send()

            @pl.when(line < GROUPS)
            def _():
                for j in range(16):
                    @pl.when(col_block != j)
                    def _():
                        ghost_copy(b, j).wait_send()

    def depthwise(b, inner):
        spans = ((3, 13),) if inner else ((0, 3), (13, 16))

        @pl.loop(0, GROUPS)
        def _(g):
            ch = group(g)
            if not inner:
                for r in range(3):
                    xrow[r, ch, :] = south[b, r, ch, :].astype(F32)
                    xrow[r + 19, ch, :] = north[b, 0, r, ch, :].astype(F32)
            xs = {r: xrow[r, ch, :] for lo, hi in spans for r in range(lo, hi + 6)}
            acc = {}
            for e in range(7):
                w = [taps[b, a * 7 + e, ch, :] for a in range(7)]
                for lo, hi in spans:
                    for q in range(lo, hi):
                        v = w[0] * xs[q]
                        for a in range(1, 7):
                            v = v + w[a] * xs[q + a]
                        if e != 3:
                            v = pltpu.roll(v, (3 - e) % 128, 1)
                        acc[q] = v if e == 0 else acc[q] + v
            for q in acc:
                conv[q, ch, :] = acc[q]

    def correct(b, inner):
        tile = diff[b]
        rows = [(q, q - 3) for q in range(3, 13)]
        if not inner:
            tile = jnp.where(
                wide_lane < 18,
                pltpu.roll(diff_s[b], 50, 1),
                jnp.where(
                    wide_lane < 54,
                    pltpu.roll(tile, 18, 1),
                    jnp.where(wide_lane < 90, pltpu.roll(tile, 122, 1), pltpu.roll(diff_n[b], 90, 1)),
                ),
            )
            rows = [(0, 0), (1, 1), (2, 2), (13, 9), (14, 10), (15, 11)]
        sums = [None] * 3
        for a in range(7):
            moved = pltpu.roll(tile, (-6 * a) % 128, 1) if a else tile
            for d in range(3):
                term = end_taps[b, a * 3 + d] * moved
                sums[d] = term if a == 0 else sums[d] + term
        fix = jnp.where(west_slot, sums[0], sums[2])
        fix = fix + jnp.where(west_slot & (place <= 1), pltpu.roll(sums[1], 127, 1), 0.0)
        fix = fix + jnp.where(~west_slot & (place >= 1), pltpu.roll(sums[1], 1, 1), 0.0)
        fix = fix + jnp.where(west_slot & (place == 0), pltpu.roll(sums[2], 126, 1), 0.0)
        fix = fix + jnp.where(~west_slot & (place == 2), pltpu.roll(sums[0], 2, 1), 0.0)
        for q, k in rows:
            conv[q] += jnp.where(row_ends, pltpu.roll(fix, (-6 * k - 3) % 128, 1), 0.0)

    def pointwise(b, first):
        @pl.loop(0, 2)
        def _(n):
            for q in range(2):
                i = first(n) + q
                parts = []
                for k in range(2):
                    cv = conv[2 * i + k]
                    mu = jnp.sum(cv, axis=0, keepdims=True) * (1.0 / 192)
                    var = jnp.sum(cv * cv, axis=0, keepdims=True) * (1.0 / 192) - mu * mu
                    parts.append(((cv - mu) * lax.rsqrt(var + 1e-6) * gain[b]).astype(BF))
                normed = jnp.concatenate(parts, axis=1)
                branch = jnp.zeros((192, 256), F32)
                for side, w in enumerate((w_own, w_other)):
                    pre = jnp.dot(w[2 * b].reshape(384, 192), normed, preferred_element_type=F32)
                    hidden = twice_gelu(pre).astype(BF)
                    branch = branch + jnp.dot(down_t[b, side], hidden, preferred_element_type=F32)
                for k in range(2):
                    r = 2 * i + k
                    new = (state[b, r].astype(F32) + 0.5 * branch[:, k * 128 : (k + 1) * 128]) * sea_rows(r)
                    if b == 0:
                        state[1, r] = new.astype(BF)
                    else:
                        out_f[pl.ds(r, 192, stride=16), :] = new

    for b in range(2):
        halo_start(b)
        depthwise(b, True)
        if b == 0:
            arrived(w_other, r_w.at[14])
            for bb in range(2):
                for side, w in enumerate((w_own, w_other)):
                    down_t[bb, side] = w[2 * bb + 1].reshape(384, 192).astype(F32).T.astype(BF)
        halo_middle(b)
        correct(b, True)
        pointwise(b, lambda n: 2 + 2 * n)
        halo_end(b)
        depthwise(b, False)
        correct(b, False)
        pointwise(b, lambda n: 6 * n)

    def chunk(l):
        chans = pl.ds(l * 24, 24)
        out_b[chans] = out_f[pl.ds(pl.multiple_of(l * 384, 384), 384), :].reshape(24, 16, 128).astype(BF)
        return out_b.at[chans]

    for i, (k, flip) in enumerate(others):
        hh = lax.rem(h + flip, 2)
        send(
            chunk(ys[k] * 2 + hh), out.at[:, my_rows, my_cols], s_o.at[i], r_o.at[lev], device(x, ys[k], hh, t, c)
        )
    last = pltpu.make_async_copy(chunk(lev), out.at[:, my_rows, my_cols], s_o.at[7])
    last.start()
    for k, flip in others:
        hh = lax.rem(h + flip, 2)
        rows, cols = cells_of(ys[k], hh)
        arrived(out.at[:, rows, cols], r_o.at[ys[k] * 2 + hh])
    last.wait()
    for cp in sends:
        cp.wait_send()
    for b in range(2):
        halo_sent(b)


def body(fields, sea_mask, fold_partner, embed_weight, dw_weight, ln_gain, up_weight, down_weight):
    partner = fold_partner.reshape(16, 128)
    hbm = pl.BlockSpec(memory_space=pl.ANY)
    dma = pltpu.SemaphoreType.DMA
    scratch = [
        pltpu.VMEM((8, 40, 16, 128), BF),
        pltpu.VMEM((16, 128), jnp.int32),
        pltpu.VMEM((16, 128), jnp.int32),
        pltpu.VMEM((40, 192), BF),
        pltpu.VMEM((2, 24, 7, 7), F32),
        pltpu.VMEM((2, 24), BF),
        pltpu.VMEM((16, 384, 128), BF),
        pltpu.VMEM((640, 128), F32),
        pltpu.VMEM((4, 2, 2, 48, 192), BF),
        pltpu.VMEM((4, 2, 2, 24, 128), F32),
        pltpu.VMEM((2, 192, 128), F32),
        pltpu.VMEM((2, 49, 192, 128), F32),
        pltpu.VMEM((2, 21, 192, 128), F32),
        pltpu.VMEM((192, 384), BF),
        pltpu.VMEM((4, 4, 2, 48, 192), BF),
        pltpu.VMEM((4, 4, 2, 48, 192), BF),
        pltpu.VMEM((2, 2, 192, 384), BF),
        pltpu.VMEM((2, 192, 128), F32),
        pltpu.VMEM((16, 192, 128), F32),
        pltpu.VMEM((2, 16, 192, 128), BF),
        pltpu.VMEM((2, 3, 192, 128), BF),
        pltpu.VMEM((2, 2, 3, 192, 128), BF),
        pltpu.VMEM((2, 192, 128), F32),
        pltpu.VMEM((2, 192, 128), F32),
        pltpu.VMEM((2, 192, 128), F32),
        pltpu.VMEM((2, 192, 128), BF),
        pltpu.VMEM((2, 192, 128), BF),
        pltpu.VMEM((2, 192, 128), BF),
        pltpu.VMEM((22, 192, 128), F32),
        pltpu.VMEM((8, 2048, 256), BF),
        pltpu.VMEM((2, 16, 3, 16, 128), BF),
        pltpu.VMEM((2, 16, 2, 3, 16, 128), BF),
        pltpu.VMEM((192 * 16, 128), F32),
        pltpu.VMEM((192, 16, 128), BF),
        dma((7,)), dma((8,)),
        dma((7,)),
        dma((12,)), dma((15,)),
        dma((2, 6)), dma((2, 6)),
        dma((2, 12)), dma((2, 16)),
        dma((2, 16)), dma((2, 12)),
        dma((8,)), dma((8,)),
    ]
    return pl.pallas_call(
        kernel,
        out_shape=jax.ShapeDtypeStruct((24, 64, 256), BF),
        in_specs=[hbm] * 8,
        out_specs=hbm,
        scratch_shapes=scratch,
        compiler_params=pltpu.CompilerParams(
            collective_id=0, has_side_effects=True, vmem_limit_bytes=60 * 1024 * 1024
        ),
    )(fields, sea_mask, partner, embed_weight, dw_weight, ln_gain, up_weight, down_weight)


def solution(mesh):
    in_specs = (
        P("lev", "gy", "gx"),
        P("gy", "gx"),
        P(),
        P("lev", None),
        P(None, "lev", None, None),
        P(None, "lev"),
        P(None, "lev", None),
        P(None, "lev", None),
    )
    out_specs = P("lev", "gy", "gx")
    return jax.shard_map(body, mesh=mesh, in_specs=in_specs, out_specs=out_specs, check_vma=False)
```

```python
import jax
import jax.numpy as jnp
from jax import lax
from jax.experimental import pallas as pl
from jax.experimental.pallas import tpu as pltpu
from jax.sharding import PartitionSpec as P

BF = jnp.bfloat16
F32 = jnp.float32
MESH = pl.DeviceIdType.MESH
GROUPS = 12


def twice_gelu(v):
    inner = v * (0.7978845608028654 + 0.035677408136300125 * (v * v))
    return v + v * jnp.tanh(inner)


def kernel(
    fields, sea, partner, embed, dw_weight, ln_gain, up, down,
    out,
    x_in, sea_in, partner_in, embed_in, dw_raw, gain_raw,
    xt, flat, pe, dw_in, dw_all, taps, end_taps, emb_t, w_own, w_other, down_t, gain, conv,
    state, south, north, diff, diff_s, diff_n, pack, from_w, from_e, xrow,
    fold_in, fold_out, fold_src, out_f, out_b,
    s_x, r_x, s_loc, s_w, r_w, s_halo, r_halo, s_f1, r_f1, s_f3, r_f3, s_o, r_o,
):
    lev = lax.axis_index("lev")
    x = lax.axis_index("gy")
    gx = lax.axis_index("gx")
    y = lev // 2
    h = lax.rem(lev, 2)
    t = gx // 2
    c = lax.rem(gx, 2)

    def row_block(yy):
        return jnp.where(lax.rem(x, 2) == 0, yy, 3 - yy)

    def half(hh):
        return lax.rem(hh + c, 2)

    def device(xx, yy, hh, tt, cc):
        return (yy * 2 + hh, xx, tt * 2 + cc)

    rb = row_block(y)
    s = half(h)
    col_block = (t * 2 + c) * 2 + s
    line = gx * 2 + h
    on_line = (x == 3) & (rb == 3)
    permutes = (x == 3) & (rb != 3) & (line < GROUPS)
    has_south = jnp.logical_not((x == 0) & (rb == 0))
    has_north = jnp.logical_not(on_line)

    outer_t = lax.rem(t + jnp.where(c == 0, 3, 1), 4)
    far = device(x, y, 1 - h, t, c)
    near = device(x, y, h, jnp.where(h == 0, outer_t, t), 1 - c)
    east_far = h == c
    east = tuple(jnp.where(east_far, f, n) for f, n in zip(far, near))
    west = tuple(jnp.where(east_far, n, f) for f, n in zip(far, near))
    step = jnp.where(lax.rem(x, 2) == 0, 1, -1)
    north_dev = device(
        jnp.where(rb == 3, jnp.minimum(x + 1, 3), x), jnp.where(rb == 3, y, jnp.clip(y + step, 0, 3)), h, t, c
    )
    south_dev = device(
        jnp.where(rb == 0, jnp.maximum(x - 1, 0), x), jnp.where(rb == 0, y, jnp.clip(y - step, 0, 3)), h, t, c
    )

    def remote(src, dst, send, recv, dev):
        return pltpu.make_async_remote_copy(
            src_ref=src, dst_ref=dst, send_sem=send, recv_sem=recv, device_id=dev, device_id_type=MESH
        )

    def arrived(dst, sem):
        remote(dst, dst, s_w.at[0], sem, far).wait_recv()

    ys = [lax.rem(y + k, 4) for k in range(4)]

    def cells_of(yy, hh):
        return (
            pl.ds(pl.multiple_of(row_block(yy) * 16, 16), 16),
            pl.ds(pl.multiple_of(half(hh) * 128, 128), 128),
        )

    my_rows, my_cols = cells_of(y, h)

    half_rows = pl.ds(pl.multiple_of(c * 48, 16), 48)
    slot = pe.at[y, h]
    dslot = dw_in.at[y, h]
    for k, ref in enumerate((up.at[0], down.at[0], up.at[1], down.at[1])):
        @pl.when(x == k)
        def _():
            pltpu.make_async_copy(ref.at[half_rows, :], slot.at[0], s_loc.at[0]).start()
    own = [
        pltpu.make_async_copy(embed, embed_in, s_loc.at[1]),
        pltpu.make_async_copy(dw_weight, dw_raw, s_loc.at[2]),
        pltpu.make_async_copy(ln_gain, gain_raw, s_loc.at[3]),
        pltpu.make_async_copy(sea.at[my_rows, my_cols], sea_in, s_loc.at[4]),
        pltpu.make_async_copy(partner, partner_in, s_loc.at[5]),
        pltpu.make_async_copy(fields.at[:, my_rows, my_cols], x_in.at[lev], s_loc.at[6]),
    ]
    for cp in own:
        cp.start()

    barrier = pltpu.get_barrier_semaphore()
    peers = [device(x, yy, 1 - h, t, c) for yy in ys]
    peers += [device(x, yy, h, t, c) for yy in ys[1:]]
    peers += [device(lax.rem(x + k, 4), y, h, t, c) for k in (1, 2, 3)]
    peers += [device(x, y, h, t, 1 - c)]

    def by_line(yy, p):
        return device(x, yy, lax.rem(p, 2), p // 4, lax.rem(p // 2, 2))

    def permuter(k, p):
        return by_line(1 + k, p)

    def rim_device(p):
        return by_line(0, p)

    def greet(dev):
        pl.semaphore_signal(barrier, inc=1, device_id=dev, device_id_type=MESH)

    for dev in peers:
        greet(dev)

    @pl.when(h == 0)
    def _():
        greet(near)

    @pl.when(on_line)
    def _():
        @pl.loop(0, GROUPS)
        def _(p):
            @pl.when(p // 2 != gx)
            def _():
                for k in range(3):
                    greet(permuter(k, p))

    @pl.when(permutes)
    def _():
        @pl.loop(0, 16)
        def _(p):
            @pl.when(p // 2 != gx)
            def _():
                greet(rim_device(p))

    own[0].wait()
    own[1].wait()
    own[2].wait()
    slot[1] = jnp.concatenate([embed_in[...].astype(F32), jnp.zeros((8, 192), F32)], axis=0).astype(BF)
    diagonal = lax.broadcasted_iota(jnp.int32, (24, 24), 0) == lax.broadcasted_iota(jnp.int32, (24, 24), 1)
    gains = gain_raw[...].astype(F32)
    for b in range(2):
        raw = dw_raw[b]
        column = jnp.sum(jnp.where(diagonal, gains[b : b + 1, :], 0.0), axis=1, keepdims=True)
        dslot[b] = jnp.concatenate(
            [raw[:, a, :] for a in range(7)] + [column, jnp.zeros((24, 78), F32)], axis=1
        )
    pltpu.make_async_copy(up.at[0].at[half_rows, :], slot.at[0], s_loc.at[0]).wait()

    across = jnp.where(on_line, jnp.where(gx < 6, 30, 36), jnp.where(permutes, 14, 0))
    pl.semaphore_wait(barrier, len(peers) + 1 - h + across)

    sends = []

    def send(src, dst, send_sem, recv_sem, dev):
        cp = remote(src, dst, send_sem, recv_sem, dev)
        cp.start()
        sends.append(cp)

    send(slot, slot, s_w.at[0], r_w.at[0], far)
    send(dslot, dslot, s_w.at[1], r_w.at[1], far)

    others = [(k, 1) for k in range(4)] + [(k, 0) for k in range(1, 4)]
    for i, (k, flip) in enumerate(others):
        hh = lax.rem(h + flip, 2)
        rows, cols = cells_of(ys[k], hh)
        send(
            fields.at[:, rows, cols], x_in.at[lev], s_x.at[i], r_x.at[lev], device(x, ys[k], hh, t, c)
        )

    arrived(pe.at[y, 1 - h], r_w.at[0])
    arrived(dw_in.at[y, 1 - h], r_w.at[1])
    for k in (1, 2, 3):
        dev = device(x, ys[k], h, t, c)
        send(pe.at[y], pe.at[y], s_w.at[2 * k], r_w.at[2 + y], dev)
        send(dw_in.at[y], dw_in.at[y], s_w.at[2 * k + 1], r_w.at[6 + y], dev)

    own[4].wait()

    for k in (1, 2, 3):
        arrived(pe.at[ys[k]], r_w.at[2 + ys[k]])
        arrived(dw_in.at[ys[k]], r_w.at[6 + ys[k]])

    for k in (1, 2, 3):
        send(
            pe.at[:, :, 0], w_own.at[x], s_w.at[7 + k], r_w.at[10 + x], device(lax.rem(x + k, 4), y, h, t, c)
        )
    w_own[x] = pe[:, :, 0]
    for l in range(8):
        for b in range(2):
            dw_all[b, l * 24 : (l + 1) * 24, :] = dw_in[l // 2, l % 2, b]
    for b in range(2):
        gain[b] = jnp.broadcast_to(dw_all[b, :, 49:50], (192, 128))
    west16 = lax.rem(lax.broadcasted_iota(jnp.int32, (16, 128), 1), 6) >= 3
    for b in range(2):
        @pl.loop(0, GROUPS)
        def _(g):
            ch = pl.ds(pl.multiple_of(g * 16, 16), 16)
            row = dw_all[b, ch, :]
            wide = [jnp.broadcast_to(row[:, k : k + 1], (16, 128)) for k in range(49)]
            for k in range(49):
                taps[b, k, ch, :] = wide[k]
            for a in range(7):
                for d in range(3):
                    end_taps[b, a * 3 + d, ch, :] = jnp.where(west16, wide[a * 7 + d], wide[a * 7 + 4 + d])

    emb_t[...] = pe[:, :, 1].reshape(384, 192).astype(F32).T.astype(BF)
    for k in (1, 2, 3):
        xk = lax.rem(x + k, 4)
        arrived(w_own.at[xk], r_w.at[10 + xk])
    send(w_own, w_other, s_w.at[11], r_w.at[14], device(x, y, h, t, 1 - c))

    own[5].wait()
    for k, flip in [(0, 0)] + others[4:] + others[:4]:
        src = ys[k] * 2 + lax.rem(h + flip, 2)
        if (k, flip) != (0, 0):
            arrived(x_in.at[src], r_x.at[src])
        flat[...] = x_in[src].astype(F32).reshape(640, 128)
        place = pl.ds(pl.multiple_of(src * 48, 16), 48)

        @pl.loop(0, 16)
        def _(r):
            part = flat[pl.ds(r, 40, stride=16), :]
            xt[r, place, :] = jnp.concatenate([part, jnp.zeros((8, 128), F32)], axis=0).astype(BF)

    own[3].wait()

    def sea_rows(r):
        return sea_in[pl.ds(r, 1), :].astype(F32)

    @pl.loop(0, 4)
    def _(n):
        for q in range(2):
            r = 4 * n + 2 * q
            both = jnp.concatenate([xt[r], xt[r + 1]], axis=1)
            stem = jnp.dot(emb_t[...], both, preferred_element_type=F32)
            state[0, r] = (stem[:, :128] * sea_rows(r)).astype(BF)
            state[0, r + 1] = (stem[:, 128:] * sea_rows(r + 1)).astype(BF)

    lane = lax.broadcasted_iota(jnp.int32, (16, 128), 1)

    wide_lane = lax.broadcasted_iota(jnp.int32, (192, 128), 1)
    west_slot = lax.rem(wide_lane, 6) >= 3
    place = lax.rem(wide_lane, 3)
    row_ends = (wide_lane < 3) | (wide_lane >= 125)

    def group(g):
        return pl.ds(pl.multiple_of(g * 16, 16), 16)

    def rim_copy(b, k, p):
        return remote(
            state.at[b, 15 - k, group(p), :], fold_in.at[b, col_block], s_f1.at[b], r_f1.at[b], permuter(k, p)
        )

    def ghost_copy(b, j):
        tj, cj, sj = j // 4, lax.rem(j // 2, 2), lax.rem(j, 2)
        return remote(
            fold_out.at[b, j], north.at[b, :, y - 1, group(line), :],
            s_f3.at[b], r_f3.at[b], device(x, 0, lax.rem(sj + cj, 2), tj, cj),
        )

    def row_copies(b):
        return (
            remote(state.at[b, pl.ds(13, 3)], south.at[b], s_halo.at[b, 0], r_halo.at[b, 0], north_dev),
            remote(state.at[b, pl.ds(0, 3)], north.at[b, 0], s_halo.at[b, 1], r_halo.at[b, 1], south_dev),
        )

    def side_copies(b):
        return (
            remote(diff.at[b], diff_s.at[b], s_halo.at[b, 4], r_halo.at[b, 4], north_dev),
            remote(diff.at[b], diff_n.at[b], s_halo.at[b, 5], r_halo.at[b, 5], south_dev),
        )

    def start_pair(pair):
        @pl.when(has_north)
        def _():
            pair[0].start()

        @pl.when(has_south)
        def _():
            pair[1].start()

    def halo_start(b):
        @pl.when(on_line)
        def _():
            @pl.loop(0, GROUPS)
            def _(p):
                for k in range(3):
                    rim_copy(b, k, p).start()

        start_pair(row_copies(b))

        @pl.loop(0, 2)
        def _(g):
            ch = pl.ds(pl.multiple_of(g * 96, 96), 96)
            lane96 = lax.broadcasted_iota(jnp.int32, (96, 128), 1)
            tile = jnp.zeros((96, 128), F32)
            for r in range(16):
                v = state[b, r, ch, :].astype(F32)
                xrow[r + 3, ch, :] = v
                tile = jnp.where((lane96 >= 6 * r) & (lane96 < 6 * r + 6), pltpu.roll(v, 6 * r + 3, 1), tile)
            pack[b, ch, :] = tile.astype(BF)

        send(pack.at[b], from_w.at[b], s_halo.at[b, 2], r_halo.at[b, 2], east)
        send(pack.at[b], from_e.at[b], s_halo.at[b, 3], r_halo.at[b, 3], west)

    def fold(b):
        arrived(fold_in.at[b], r_f1.at[b])
        for j in range(16):
            fold_src[j] = fold_in[b, j].astype(F32)

        ghosts = []
        for j in range(16):
            column = jnp.broadcast_to(partner_in[j : j + 1, :], (16, 128))
            within, block = column & 127, column >> 7
            picked = [jnp.take_along_axis(fold_src[i], within, axis=1) for i in range(16)]
            for bit in range(4):
                odd = ((block >> bit) & 1) == 1
                picked = [jnp.where(odd, picked[i + 1], picked[i]) for i in range(0, len(picked), 2)]
            ghosts.append(picked[0])
        for j in range(16):
            fold_out[b, j, 0] = ghosts[j].astype(BF)
            fold_out[b, j, 1] = jnp.where(lane < 64, ghosts[(j + 1) % 16], ghosts[j - 1]).astype(BF)

        @pl.loop(0, 16)
        def _(j):
            ghost_copy(b, j).start()

    def halo_middle(b):
        arrived(from_w.at[b], r_halo.at[b, 2])
        arrived(from_e.at[b], r_halo.at[b, 3])
        mine = pack[b].astype(F32)
        diff[b] = jnp.where(
            west_slot,
            pltpu.roll(from_w[b].astype(F32) - mine, 3, 1),
            pltpu.roll(from_e[b].astype(F32) - mine, 125, 1),
        )
        start_pair(side_copies(b))

        @pl.when(permutes)
        def _():
            fold(b)

    def south_in(b):
        @pl.when(has_south)
        def _():
            arrived(south.at[b], r_halo.at[b, 0])
            arrived(diff_s.at[b], r_halo.at[b, 4])

        @pl.when(jnp.logical_not(has_south))
        def _():
            south[b] = jnp.zeros((3, 192, 128), BF)
            diff_s[b] = jnp.zeros((192, 128), F32)

    def north_in(b):
        @pl.when(has_north)
        def _():
            arrived(north.at[b, 0], r_halo.at[b, 1])
            arrived(diff_n.at[b], r_halo.at[b, 5])

        @pl.when(on_line)
        def _():
            arrived(north.at[b], r_f3.at[b])

            @pl.loop(0, GROUPS)
            def _(g):
                ch = group(g)
                tile = jnp.zeros((16, 128), F32)
                for r in range(3):
                    d = north[b, 1, r, ch, :].astype(F32) - north[b, 0, r, ch, :].astype(F32)
                    tile = jnp.where((lane >= 6 * r) & (lane < 6 * r + 3), pltpu.roll(d, 6 * r, 1), tile)
                    tile = jnp.where(
                        (lane >= 6 * r + 3) & (lane < 6 * r + 6), pltpu.roll(d, 6 * r + 6, 1), tile
                    )
                diff_n[b, ch, :] = tile

    def halo_sent(b):
        for pair in (row_copies(b), side_copies(b)):
            @pl.when(has_north)
            def _():
                pair[0].wait_send()

            @pl.when(has_south)
            def _():
                pair[1].wait_send()

        @pl.when(on_line)
        def _():
            rim = state.at[b, pl.ds(13, 3)]
            remote(rim, rim, s_f1.at[b], r_f1.at[b], far).wait_send()

        @pl.when(permutes)
        def _():
            remote(fold_out.at[b], fold_out.at[b], s_f3.at[b], r_f3.at[b], far).wait_send()

    def depthwise(b, lo, hi):
        @pl.loop(0, GROUPS)
        def _(g):
            ch = group(g)
            for r in range(3):
                if lo == 0:
                    xrow[r, ch, :] = south[b, r, ch, :].astype(F32)
                if hi == 16:
                    xrow[r + 19, ch, :] = north[b, 0, r, ch, :].astype(F32)
            xs = {r: xrow[r, ch, :] for r in range(lo, hi + 6)}
            acc = {}
            for e in range(7):
                w = [taps[b, a * 7 + e, ch, :] for a in range(7)]
                for q in range(lo, hi):
                    v = w[0] * xs[q]
                    for a in range(1, 7):
                        v = v + w[a] * xs[q + a]
                    if e != 3:
                        v = pltpu.roll(v, (3 - e) % 128, 1)
                    acc[q] = v if e == 0 else acc[q] + v
            for q in acc:
                conv[q, ch, :] = acc[q]

    def correct(b, lo, hi):
        tile = diff[b]
        if lo == 0:
            tile = jnp.where(wide_lane < 18, pltpu.roll(diff_s[b], 50, 1), pltpu.roll(tile, 18, 1))
        elif hi == 16:
            tile = jnp.where(wide_lane < 36, pltpu.roll(tile, 68, 1), pltpu.roll(diff_n[b], 36, 1))
        sums = [None] * 3
        for a in range(7):
            moved = pltpu.roll(tile, (-6 * a) % 128, 1) if a else tile
            for d in range(3):
                term = end_taps[b, a * 3 + d] * moved
                sums[d] = term if a == 0 else sums[d] + term
        fix = jnp.where(west_slot, sums[0], sums[2])
        fix = fix + jnp.where(west_slot & (place <= 1), pltpu.roll(sums[1], 127, 1), 0.0)
        fix = fix + jnp.where(~west_slot & (place >= 1), pltpu.roll(sums[1], 1, 1), 0.0)
        fix = fix + jnp.where(west_slot & (place == 0), pltpu.roll(sums[2], 126, 1), 0.0)
        fix = fix + jnp.where(~west_slot & (place == 2), pltpu.roll(sums[0], 2, 1), 0.0)
        for q in range(lo, hi):
            conv[q] += jnp.where(row_ends, pltpu.roll(fix, (-6 * (q - lo) - 3) % 128, 1), 0.0)

    def pointwise(b, first):
        for q in range(2):
            i = first + q
            parts = []
            for k in range(2):
                cv = conv[2 * i + k]
                mu = jnp.sum(cv, axis=0, keepdims=True) * (1.0 / 192)
                var = jnp.sum(cv * cv, axis=0, keepdims=True) * (1.0 / 192) - mu * mu
                parts.append(((cv - mu) * lax.rsqrt(var + 1e-6) * gain[b]).astype(BF))
            normed = jnp.concatenate(parts, axis=1)
            branch = jnp.zeros((192, 256), F32)
            for side, w in enumerate((w_own, w_other)):
                pre = jnp.dot(w[2 * b].reshape(384, 192), normed, preferred_element_type=F32)
                hidden = twice_gelu(pre).astype(BF)
                branch = branch + jnp.dot(down_t[b, side], hidden, preferred_element_type=F32)
            for k in range(2):
                r = 2 * i + k
                new = (state[b, r].astype(F32) + 0.5 * branch[:, k * 128 : (k + 1) * 128]) * sea_rows(r)
                if b == 0:
                    state[1, r] = new.astype(BF)
                else:
                    out_f[pl.ds(r, 192, stride=16), :] = new

    for b in range(2):
        halo_start(b)
        depthwise(b, 3, 13)
        if b == 0:
            arrived(w_other, r_w.at[14])
            for bb in range(2):
                for side, w in enumerate((w_own, w_other)):
                    down_t[bb, side] = w[2 * bb + 1].reshape(384, 192).astype(F32).T.astype(BF)
        halo_middle(b)
        correct(b, 3, 13)

        @pl.loop(0, 2)
        def _(n):
            pointwise(b, 2 + 2 * n)

        south_in(b)
        depthwise(b, 0, 3)
        correct(b, 0, 3)
        pointwise(b, 0)
        north_in(b)
        depthwise(b, 13, 16)
        correct(b, 13, 16)
        pointwise(b, 6)

    def chunk(l):
        chans = pl.ds(l * 24, 24)
        out_b[chans] = out_f[pl.ds(pl.multiple_of(l * 384, 384), 384), :].reshape(24, 16, 128).astype(BF)
        return out_b.at[chans]

    for i, (k, flip) in enumerate(others):
        hh = lax.rem(h + flip, 2)
        send(
            chunk(ys[k] * 2 + hh), out.at[:, my_rows, my_cols], s_o.at[i], r_o.at[lev], device(x, ys[k], hh, t, c)
        )
    last = pltpu.make_async_copy(chunk(lev), out.at[:, my_rows, my_cols], s_o.at[7])
    last.start()
    for k, flip in others:
        hh = lax.rem(h + flip, 2)
        rows, cols = cells_of(ys[k], hh)
        arrived(out.at[:, rows, cols], r_o.at[ys[k] * 2 + hh])
    last.wait()
    for cp in sends:
        cp.wait_send()
    for b in range(2):
        halo_sent(b)


def body(fields, sea_mask, fold_partner, embed_weight, dw_weight, ln_gain, up_weight, down_weight):
    partner = fold_partner.reshape(16, 128)
    hbm = pl.BlockSpec(memory_space=pl.ANY)
    dma = pltpu.SemaphoreType.DMA
    scratch = [
        pltpu.VMEM((8, 40, 16, 128), BF),
        pltpu.VMEM((16, 128), jnp.int32),
        pltpu.VMEM((16, 128), jnp.int32),
        pltpu.VMEM((40, 192), BF),
        pltpu.VMEM((2, 24, 7, 7), F32),
        pltpu.VMEM((2, 24), BF),
        pltpu.VMEM((16, 384, 128), BF),
        pltpu.VMEM((640, 128), F32),
        pltpu.VMEM((4, 2, 2, 48, 192), BF),
        pltpu.VMEM((4, 2, 2, 24, 128), F32),
        pltpu.VMEM((2, 192, 128), F32),
        pltpu.VMEM((2, 49, 192, 128), F32),
        pltpu.VMEM((2, 21, 192, 128), F32),
        pltpu.VMEM((192, 384), BF),
        pltpu.VMEM((4, 4, 2, 48, 192), BF),
        pltpu.VMEM((4, 4, 2, 48, 192), BF),
        pltpu.VMEM((2, 2, 192, 384), BF),
        pltpu.VMEM((2, 192, 128), F32),
        pltpu.VMEM((16, 192, 128), F32),
        pltpu.VMEM((2, 16, 192, 128), BF),
        pltpu.VMEM((2, 3, 192, 128), BF),
        pltpu.VMEM((2, 2, 3, 192, 128), BF),
        pltpu.VMEM((2, 192, 128), F32),
        pltpu.VMEM((2, 192, 128), F32),
        pltpu.VMEM((2, 192, 128), F32),
        pltpu.VMEM((2, 192, 128), BF),
        pltpu.VMEM((2, 192, 128), BF),
        pltpu.VMEM((2, 192, 128), BF),
        pltpu.VMEM((22, 192, 128), F32),
        pltpu.VMEM((2, 16, 16, 128), BF),
        pltpu.VMEM((2, 16, 2, 16, 128), BF),
        pltpu.VMEM((16, 16, 128), F32),
        pltpu.VMEM((192 * 16, 128), F32),
        pltpu.VMEM((192, 16, 128), BF),
        dma((7,)), dma((8,)),
        dma((7,)),
        dma((12,)), dma((15,)),
        dma((2, 6)), dma((2, 6)),
        dma((2,)), dma((2,)),
        dma((2,)), dma((2,)),
        dma((8,)), dma((8,)),
    ]
    return pl.pallas_call(
        kernel,
        out_shape=jax.ShapeDtypeStruct((24, 64, 256), BF),
        in_specs=[hbm] * 8,
        out_specs=hbm,
        scratch_shapes=scratch,
        compiler_params=pltpu.CompilerParams(
            collective_id=0, has_side_effects=True, vmem_limit_bytes=60 * 1024 * 1024
        ),
    )(fields, sea_mask, partner, embed_weight, dw_weight, ln_gain, up_weight, down_weight)


def solution(mesh):
    in_specs = (
        P("lev", "gy", "gx"),
        P("gy", "gx"),
        P(),
        P("lev", None),
        P(None, "lev", None, None),
        P(None, "lev"),
        P(None, "lev", None),
        P(None, "lev", None),
    )
    out_specs = P("lev", "gy", "gx")
    return jax.shard_map(body, mesh=mesh, in_specs=in_specs, out_specs=out_specs, check_vma=False)
```

```python
import jax
import jax.numpy as jnp
from jax import lax
from jax.experimental import pallas as pl
from jax.experimental.pallas import tpu as pltpu
from jax.sharding import PartitionSpec as P

BF = jnp.bfloat16
F32 = jnp.float32
MESH = pl.DeviceIdType.MESH
GROUPS = 12


def twice_gelu(v):
    inner = v * (0.7978845608028654 + 0.035677408136300125 * (v * v))
    return v + v * jnp.tanh(inner)


def kernel(
    fields, sea, partner, embed, dw_weight, ln_gain, up, down,
    out,
    x_in, sea_in, partner_in, embed_in, dw_raw, gain_raw,
    xt, flat, pe, dw_in, dw_all, taps, end_taps, emb_t, w_own, w_other, down_t, gain, conv,
    state, south, north, diff, diff_s, diff_n, pack, from_w, from_e, xrow,
    fold_in, fold_out, fold_src, out_f, out_b,
    s_x, r_x, s_loc, s_w, r_w, s_halo, r_halo, s_f1, r_f1, s_f3, r_f3, s_o, r_o,
):
    lev = lax.axis_index("lev")
    x = lax.axis_index("gy")
    gx = lax.axis_index("gx")
    y = lev // 2
    h = lax.rem(lev, 2)
    t = gx // 2
    c = lax.rem(gx, 2)

    def row_block(yy):
        return jnp.where(lax.rem(x, 2) == 0, yy, 3 - yy)

    def half(hh):
        return lax.rem(hh + c, 2)

    def device(xx, yy, hh, tt, cc):
        return (yy * 2 + hh, xx, tt * 2 + cc)

    rb = row_block(y)
    s = half(h)
    col_block = (t * 2 + c) * 2 + s
    line = gx * 2 + h
    on_line = (x == 3) & (rb == 3)
    permutes = (x == 3) & (rb != 3) & (line < GROUPS)
    has_south = jnp.logical_not((x == 0) & (rb == 0))
    has_north = jnp.logical_not(on_line)

    outer_t = lax.rem(t + jnp.where(c == 0, 3, 1), 4)
    far = device(x, y, 1 - h, t, c)
    near = device(x, y, h, jnp.where(h == 0, outer_t, t), 1 - c)
    east_far = h == c
    east = tuple(jnp.where(east_far, f, n) for f, n in zip(far, near))
    west = tuple(jnp.where(east_far, n, f) for f, n in zip(far, near))
    step = jnp.where(lax.rem(x, 2) == 0, 1, -1)
    north_dev = device(
        jnp.where(rb == 3, jnp.minimum(x + 1, 3), x), jnp.where(rb == 3, y, jnp.clip(y + step, 0, 3)), h, t, c
    )
    south_dev = device(
        jnp.where(rb == 0, jnp.maximum(x - 1, 0), x), jnp.where(rb == 0, y, jnp.clip(y - step, 0, 3)), h, t, c
    )

    def remote(src, dst, send, recv, dev):
        return pltpu.make_async_remote_copy(
            src_ref=src, dst_ref=dst, send_sem=send, recv_sem=recv, device_id=dev, device_id_type=MESH
        )

    def arrived(dst, sem):
        remote(dst, dst, s_w.at[0], sem, far).wait_recv()

    ys = [lax.rem(y + k, 4) for k in range(4)]

    def cells_of(yy, hh):
        return (
            pl.ds(pl.multiple_of(row_block(yy) * 16, 16), 16),
            pl.ds(pl.multiple_of(half(hh) * 128, 128), 128),
        )

    my_rows, my_cols = cells_of(y, h)

    half_rows = pl.ds(pl.multiple_of(c * 48, 16), 48)
    slot = pe.at[y, h]
    dslot = dw_in.at[y, h]
    for k, ref in enumerate((up.at[0], down.at[0], up.at[1], down.at[1])):
        @pl.when(x == k)
        def _():
            pltpu.make_async_copy(ref.at[half_rows, :], slot.at[0], s_loc.at[0]).start()
    own = [
        pltpu.make_async_copy(embed, embed_in, s_loc.at[1]),
        pltpu.make_async_copy(dw_weight, dw_raw, s_loc.at[2]),
        pltpu.make_async_copy(ln_gain, gain_raw, s_loc.at[3]),
        pltpu.make_async_copy(sea.at[my_rows, my_cols], sea_in, s_loc.at[4]),
        pltpu.make_async_copy(partner, partner_in, s_loc.at[5]),
        pltpu.make_async_copy(fields.at[:, my_rows, my_cols], x_in.at[lev], s_loc.at[6]),
    ]
    for cp in own:
        cp.start()

    barrier = pltpu.get_barrier_semaphore()
    peers = [device(x, yy, 1 - h, t, c) for yy in ys]
    peers += [device(x, yy, h, t, c) for yy in ys[1:]]
    peers += [device(lax.rem(x + k, 4), y, h, t, c) for k in (1, 2, 3)]
    peers += [device(x, y, h, t, 1 - c)]

    def by_line(yy, p):
        return device(x, yy, lax.rem(p, 2), p // 4, lax.rem(p // 2, 2))

    def permuter(k, p):
        return by_line(1 + k, p)

    def rim_device(p):
        return by_line(0, p)

    def greet(dev):
        pl.semaphore_signal(barrier, inc=1, device_id=dev, device_id_type=MESH)

    for dev in peers:
        greet(dev)

    @pl.when(h == 0)
    def _():
        greet(near)

    @pl.when(on_line)
    def _():
        @pl.loop(0, GROUPS)
        def _(p):
            @pl.when(p // 2 != gx)
            def _():
                for k in range(3):
                    greet(permuter(k, p))

    @pl.when(permutes)
    def _():
        @pl.loop(0, 16)
        def _(p):
            @pl.when(p // 2 != gx)
            def _():
                greet(rim_device(p))

    own[0].wait()
    own[1].wait()
    own[2].wait()
    slot[1] = jnp.concatenate([embed_in[...].astype(F32), jnp.zeros((8, 192), F32)], axis=0).astype(BF)
    diagonal = lax.broadcasted_iota(jnp.int32, (24, 24), 0) == lax.broadcasted_iota(jnp.int32, (24, 24), 1)
    gains = gain_raw[...].astype(F32)
    for b in range(2):
        raw = dw_raw[b]
        column = jnp.sum(jnp.where(diagonal, gains[b : b + 1, :], 0.0), axis=1, keepdims=True)
        dslot[b] = jnp.concatenate(
            [raw[:, a, :] for a in range(7)] + [column, jnp.zeros((24, 78), F32)], axis=1
        )
    pltpu.make_async_copy(up.at[0].at[half_rows, :], slot.at[0], s_loc.at[0]).wait()

    across = jnp.where(on_line, jnp.where(gx < 6, 30, 36), jnp.where(permutes, 14, 0))
    pl.semaphore_wait(barrier, len(peers) + 1 - h + across)

    sends = []

    def send(src, dst, send_sem, recv_sem, dev):
        cp = remote(src, dst, send_sem, recv_sem, dev)
        cp.start()
        sends.append(cp)

    send(slot, slot, s_w.at[0], r_w.at[0], far)
    send(dslot, dslot, s_w.at[1], r_w.at[1], far)

    others = [(k, 1) for k in range(4)] + [(k, 0) for k in range(1, 4)]
    for i, (k, flip) in enumerate(others):
        hh = lax.rem(h + flip, 2)
        rows, cols = cells_of(ys[k], hh)
        send(
            fields.at[:, rows, cols], x_in.at[lev], s_x.at[i], r_x.at[lev], device(x, ys[k], hh, t, c)
        )

    arrived(pe.at[y, 1 - h], r_w.at[0])
    arrived(dw_in.at[y, 1 - h], r_w.at[1])
    for k in (1, 2, 3):
        dev = device(x, ys[k], h, t, c)
        send(pe.at[y], pe.at[y], s_w.at[2 * k], r_w.at[2 + y], dev)
        send(dw_in.at[y], dw_in.at[y], s_w.at[2 * k + 1], r_w.at[6 + y], dev)

    own[4].wait()

    for k in (1, 2, 3):
        arrived(pe.at[ys[k]], r_w.at[2 + ys[k]])
        arrived(dw_in.at[ys[k]], r_w.at[6 + ys[k]])

    for k in (1, 2, 3):
        send(
            pe.at[:, :, 0], w_own.at[x], s_w.at[7 + k], r_w.at[10 + x], device(lax.rem(x + k, 4), y, h, t, c)
        )
    w_own[x] = pe[:, :, 0]
    for l in range(8):
        for b in range(2):
            dw_all[b, l * 24 : (l + 1) * 24, :] = dw_in[l // 2, l % 2, b]
    for b in range(2):
        gain[b] = jnp.broadcast_to(dw_all[b, :, 49:50], (192, 128))
    west16 = lax.rem(lax.broadcasted_iota(jnp.int32, (16, 128), 1), 6) >= 3
    for b in range(2):
        @pl.loop(0, GROUPS)
        def _(g):
            ch = pl.ds(pl.multiple_of(g * 16, 16), 16)
            row = dw_all[b, ch, :]
            wide = [jnp.broadcast_to(row[:, k : k + 1], (16, 128)) for k in range(49)]
            for k in range(49):
                taps[b, k, ch, :] = wide[k]
            for a in range(7):
                for d in range(3):
                    end_taps[b, a * 3 + d, ch, :] = jnp.where(west16, wide[a * 7 + d], wide[a * 7 + 4 + d])

    emb_t[...] = pe[:, :, 1].reshape(384, 192).astype(F32).T.astype(BF)
    for k in (1, 2, 3):
        xk = lax.rem(x + k, 4)
        arrived(w_own.at[xk], r_w.at[10 + xk])
    send(w_own, w_other, s_w.at[11], r_w.at[14], device(x, y, h, t, 1 - c))

    own[5].wait()
    for k, flip in [(0, 0)] + others[4:] + others[:4]:
        src = ys[k] * 2 + lax.rem(h + flip, 2)
        if (k, flip) != (0, 0):
            arrived(x_in.at[src], r_x.at[src])
        flat[...] = x_in[src].astype(F32).reshape(640, 128)
        place = pl.ds(pl.multiple_of(src * 48, 16), 48)

        @pl.loop(0, 16)
        def _(r):
            part = flat[pl.ds(r, 40, stride=16), :]
            xt[r, place, :] = jnp.concatenate([part, jnp.zeros((8, 128), F32)], axis=0).astype(BF)

    own[3].wait()

    def sea_rows(r):
        return sea_in[pl.ds(r, 1), :].astype(F32)

    @pl.loop(0, 4)
    def _(n):
        for q in range(2):
            r = 4 * n + 2 * q
            both = jnp.concatenate([xt[r], xt[r + 1]], axis=1)
            stem = jnp.dot(emb_t[...], both, preferred_element_type=F32)
            state[0, r] = (stem[:, :128] * sea_rows(r)).astype(BF)
            state[0, r + 1] = (stem[:, 128:] * sea_rows(r + 1)).astype(BF)

    lane = lax.broadcasted_iota(jnp.int32, (16, 128), 1)

    wide_lane = lax.broadcasted_iota(jnp.int32, (192, 128), 1)
    west_slot = lax.rem(wide_lane, 6) >= 3
    place = lax.rem(wide_lane, 3)
    row_ends = (wide_lane < 3) | (wide_lane >= 125)

    def group(g):
        return pl.ds(pl.multiple_of(g * 16, 16), 16)

    def rim_copy(b, k, p):
        return remote(
            state.at[b, 15 - k, group(p), :], fold_in.at[b, col_block], s_f1.at[b], r_f1.at[b], permuter(k, p)
        )

    def ghost_copy(b, j):
        tj, cj, sj = j // 4, lax.rem(j // 2, 2), lax.rem(j, 2)
        return remote(
            fold_out.at[b, j], north.at[b, :, y - 1, group(line), :],
            s_f3.at[b], r_f3.at[b], device(x, 0, lax.rem(sj + cj, 2), tj, cj),
        )

    def row_copies(b):
        return (
            remote(state.at[b, pl.ds(13, 3)], south.at[b], s_halo.at[b, 0], r_halo.at[b, 0], north_dev),
            remote(state.at[b, pl.ds(0, 3)], north.at[b, 0], s_halo.at[b, 1], r_halo.at[b, 1], south_dev),
        )

    def side_copies(b):
        return (
            remote(diff.at[b], diff_s.at[b], s_halo.at[b, 4], r_halo.at[b, 4], north_dev),
            remote(diff.at[b], diff_n.at[b], s_halo.at[b, 5], r_halo.at[b, 5], south_dev),
        )

    def pack_copies(b):
        return (
            remote(pack.at[b], from_w.at[b], s_halo.at[b, 2], r_halo.at[b, 2], east),
            remote(pack.at[b], from_e.at[b], s_halo.at[b, 3], r_halo.at[b, 3], west),
        )

    def start_pair(pair):
        @pl.when(has_north)
        def _():
            pair[0].start()

        @pl.when(has_south)
        def _():
            pair[1].start()

    def halo_start(b):
        @pl.when(on_line)
        def _():
            @pl.loop(0, GROUPS)
            def _(p):
                for k in range(3):
                    rim_copy(b, k, p).start()

        start_pair(row_copies(b))

        @pl.loop(0, 2)
        def _(g):
            ch = pl.ds(pl.multiple_of(g * 96, 96), 96)
            lane96 = lax.broadcasted_iota(jnp.int32, (96, 128), 1)
            tile = jnp.zeros((96, 128), F32)
            for r in range(16):
                v = state[b, r, ch, :].astype(F32)
                xrow[r + 3, ch, :] = v
                tile = jnp.where((lane96 >= 6 * r) & (lane96 < 6 * r + 6), pltpu.roll(v, 6 * r + 3, 1), tile)
            pack[b, ch, :] = tile.astype(BF)

        for cp in pack_copies(b):
            cp.start()

    def fold(b):
        arrived(fold_in.at[b], r_f1.at[b])
        for j in range(16):
            fold_src[j] = fold_in[b, j].astype(F32)

        ghosts = []
        for j in range(16):
            column = jnp.broadcast_to(partner_in[j : j + 1, :], (16, 128))
            within, block = column & 127, column >> 7
            picked = [jnp.take_along_axis(fold_src[i], within, axis=1) for i in range(16)]
            for bit in range(4):
                odd = ((block >> bit) & 1) == 1
                picked = [jnp.where(odd, picked[i + 1], picked[i]) for i in range(0, len(picked), 2)]
            ghosts.append(picked[0])
        for j in range(16):
            fold_out[b, j, 0] = ghosts[j].astype(BF)
            fold_out[b, j, 1] = jnp.where(lane < 64, ghosts[(j + 1) % 16], ghosts[j - 1]).astype(BF)

        @pl.loop(0, 16)
        def _(j):
            ghost_copy(b, j).start()

    def halo_middle(b):
        arrived(from_w.at[b], r_halo.at[b, 2])
        arrived(from_e.at[b], r_halo.at[b, 3])
        mine = pack[b].astype(F32)
        diff[b] = jnp.where(
            west_slot,
            pltpu.roll(from_w[b].astype(F32) - mine, 3, 1),
            pltpu.roll(from_e[b].astype(F32) - mine, 125, 1),
        )
        start_pair(side_copies(b))

        @pl.when(permutes)
        def _():
            fold(b)

    def south_in(b):
        @pl.when(has_south)
        def _():
            arrived(south.at[b], r_halo.at[b, 0])
            arrived(diff_s.at[b], r_halo.at[b, 4])

        @pl.when(jnp.logical_not(has_south))
        def _():
            south[b] = jnp.zeros((3, 192, 128), BF)
            diff_s[b] = jnp.zeros((192, 128), F32)

    def north_in(b):
        @pl.when(has_north)
        def _():
            arrived(north.at[b, 0], r_halo.at[b, 1])
            arrived(diff_n.at[b], r_halo.at[b, 5])

        @pl.when(on_line)
        def _():
            arrived(north.at[b], r_f3.at[b])

            @pl.loop(0, GROUPS)
            def _(g):
                ch = group(g)
                tile = jnp.zeros((16, 128), F32)
                for r in range(3):
                    d = north[b, 1, r, ch, :].astype(F32) - north[b, 0, r, ch, :].astype(F32)
                    tile = jnp.where((lane >= 6 * r) & (lane < 6 * r + 3), pltpu.roll(d, 6 * r, 1), tile)
                    tile = jnp.where(
                        (lane >= 6 * r + 3) & (lane < 6 * r + 6), pltpu.roll(d, 6 * r + 6, 1), tile
                    )
                diff_n[b, ch, :] = tile

    def halo_sent(b):
        for cp in pack_copies(b):
            cp.wait_send()

        for pair in (row_copies(b), side_copies(b)):
            @pl.when(has_north)
            def _():
                pair[0].wait_send()

            @pl.when(has_south)
            def _():
                pair[1].wait_send()

        @pl.when(on_line)
        def _():
            rim = state.at[b, pl.ds(13, 3)]
            remote(rim, rim, s_f1.at[b], r_f1.at[b], far).wait_send()

        @pl.when(permutes)
        def _():
            remote(fold_out.at[b], fold_out.at[b], s_f3.at[b], r_f3.at[b], far).wait_send()

    def depthwise(b, lo, hi):
        @pl.loop(0, GROUPS)
        def _(g):
            ch = group(g)
            for r in range(3):
                if lo == 0:
                    xrow[r, ch, :] = south[b, r, ch, :].astype(F32)
                if hi == 16:
                    xrow[r + 19, ch, :] = north[b, 0, r, ch, :].astype(F32)
            xs = {r: xrow[r, ch, :] for r in range(lo, hi + 6)}
            acc = {}
            for e in range(7):
                w = [taps[b, a * 7 + e, ch, :] for a in range(7)]
                for q in range(lo, hi):
                    v = w[0] * xs[q]
                    for a in range(1, 7):
                        v = v + w[a] * xs[q + a]
                    if e != 3:
                        v = pltpu.roll(v, (3 - e) % 128, 1)
                    acc[q] = v if e == 0 else acc[q] + v
            for q in acc:
                conv[q, ch, :] = acc[q]

    def correct(b, lo, hi):
        tile = diff[b]
        if lo == 0:
            tile = jnp.where(wide_lane < 18, pltpu.roll(diff_s[b], 50, 1), pltpu.roll(tile, 18, 1))
        elif hi == 16:
            tile = jnp.where(wide_lane < 36, pltpu.roll(tile, 68, 1), pltpu.roll(diff_n[b], 36, 1))
        sums = [None] * 3
        for a in range(7):
            moved = pltpu.roll(tile, (-6 * a) % 128, 1) if a else tile
            for d in range(3):
                term = end_taps[b, a * 3 + d] * moved
                sums[d] = term if a == 0 else sums[d] + term
        fix = jnp.where(west_slot, sums[0], sums[2])
        fix = fix + jnp.where(west_slot & (place <= 1), pltpu.roll(sums[1], 127, 1), 0.0)
        fix = fix + jnp.where(~west_slot & (place >= 1), pltpu.roll(sums[1], 1, 1), 0.0)
        fix = fix + jnp.where(west_slot & (place == 0), pltpu.roll(sums[2], 126, 1), 0.0)
        fix = fix + jnp.where(~west_slot & (place == 2), pltpu.roll(sums[0], 2, 1), 0.0)
        for q in range(lo, hi):
            conv[q] += jnp.where(row_ends, pltpu.roll(fix, (-6 * (q - lo) - 3) % 128, 1), 0.0)

    def pointwise(b, first):
        for q in range(2):
            i = first + q
            parts = []
            for k in range(2):
                cv = conv[2 * i + k]
                mu = jnp.sum(cv, axis=0, keepdims=True) * (1.0 / 192)
                var = jnp.sum(cv * cv, axis=0, keepdims=True) * (1.0 / 192) - mu * mu
                parts.append(((cv - mu) * lax.rsqrt(var + 1e-6) * gain[b]).astype(BF))
            normed = jnp.concatenate(parts, axis=1)
            branch = jnp.zeros((192, 256), F32)
            for side, w in enumerate((w_own, w_other)):
                pre = jnp.dot(w[2 * b].reshape(384, 192), normed, preferred_element_type=F32)
                hidden = twice_gelu(pre).astype(BF)
                branch = branch + jnp.dot(down_t[b, side], hidden, preferred_element_type=F32)
            for k in range(2):
                r = 2 * i + k
                new = (state[b, r].astype(F32) + 0.5 * branch[:, k * 128 : (k + 1) * 128]) * sea_rows(r)
                state[b + 1, r] = new.astype(BF)
                out_f[pl.ds(r, 192, stride=16), :] = new

    @pl.loop(0, 2)
    def _(b):
        halo_start(b)
        depthwise(b, 3, 13)

        @pl.when(b == 0)
        def _():
            arrived(w_other, r_w.at[14])

        for side, w in enumerate((w_own, w_other)):
            down_t[b, side] = w[2 * b + 1].reshape(384, 192).astype(F32).T.astype(BF)

        halo_middle(b)
        correct(b, 3, 13)

        @pl.loop(0, 2)
        def _(n):
            pointwise(b, 2 + 2 * n)

        south_in(b)
        depthwise(b, 0, 3)
        correct(b, 0, 3)
        pointwise(b, 0)
        north_in(b)
        depthwise(b, 13, 16)
        correct(b, 13, 16)
        pointwise(b, 6)

    def chunk(l):
        chans = pl.ds(l * 24, 24)
        out_b[chans] = out_f[pl.ds(pl.multiple_of(l * 384, 384), 384), :].reshape(24, 16, 128).astype(BF)
        return out_b.at[chans]

    for i, (k, flip) in enumerate(others):
        hh = lax.rem(h + flip, 2)
        send(
            chunk(ys[k] * 2 + hh), out.at[:, my_rows, my_cols], s_o.at[i], r_o.at[lev], device(x, ys[k], hh, t, c)
        )
    last = pltpu.make_async_copy(chunk(lev), out.at[:, my_rows, my_cols], s_o.at[7])
    last.start()
    for k, flip in others:
        hh = lax.rem(h + flip, 2)
        rows, cols = cells_of(ys[k], hh)
        arrived(out.at[:, rows, cols], r_o.at[ys[k] * 2 + hh])
    last.wait()
    for cp in sends:
        cp.wait_send()
    @pl.loop(0, 2)
    def _(b):
        halo_sent(b)


def body(fields, sea_mask, fold_partner, embed_weight, dw_weight, ln_gain, up_weight, down_weight):
    partner = fold_partner.reshape(16, 128)
    hbm = pl.BlockSpec(memory_space=pl.ANY)
    dma = pltpu.SemaphoreType.DMA
    scratch = [
        pltpu.VMEM((8, 40, 16, 128), BF),
        pltpu.VMEM((16, 128), jnp.int32),
        pltpu.VMEM((16, 128), jnp.int32),
        pltpu.VMEM((40, 192), BF),
        pltpu.VMEM((2, 24, 7, 7), F32),
        pltpu.VMEM((2, 24), BF),
        pltpu.VMEM((16, 384, 128), BF),
        pltpu.VMEM((640, 128), F32),
        pltpu.VMEM((4, 2, 2, 48, 192), BF),
        pltpu.VMEM((4, 2, 2, 24, 128), F32),
        pltpu.VMEM((2, 192, 128), F32),
        pltpu.VMEM((2, 49, 192, 128), F32),
        pltpu.VMEM((2, 21, 192, 128), F32),
        pltpu.VMEM((192, 384), BF),
        pltpu.VMEM((4, 4, 2, 48, 192), BF),
        pltpu.VMEM((4, 4, 2, 48, 192), BF),
        pltpu.VMEM((2, 2, 192, 384), BF),
        pltpu.VMEM((2, 192, 128), F32),
        pltpu.VMEM((16, 192, 128), F32),
        pltpu.VMEM((3, 16, 192, 128), BF),
        pltpu.VMEM((2, 3, 192, 128), BF),
        pltpu.VMEM((2, 2, 3, 192, 128), BF),
        pltpu.VMEM((2, 192, 128), F32),
        pltpu.VMEM((2, 192, 128), F32),
        pltpu.VMEM((2, 192, 128), F32),
        pltpu.VMEM((2, 192, 128), BF),
        pltpu.VMEM((2, 192, 128), BF),
        pltpu.VMEM((2, 192, 128), BF),
        pltpu.VMEM((22, 192, 128), F32),
        pltpu.VMEM((2, 16, 16, 128), BF),
        pltpu.VMEM((2, 16, 2, 16, 128), BF),
        pltpu.VMEM((16, 16, 128), F32),
        pltpu.VMEM((192 * 16, 128), F32),
        pltpu.VMEM((192, 16, 128), BF),
        dma((7,)), dma((8,)),
        dma((7,)),
        dma((12,)), dma((15,)),
        dma((2, 6)), dma((2, 6)),
        dma((2,)), dma((2,)),
        dma((2,)), dma((2,)),
        dma((8,)), dma((8,)),
    ]
    return pl.pallas_call(
        kernel,
        out_shape=jax.ShapeDtypeStruct((24, 64, 256), BF),
        in_specs=[hbm] * 8,
        out_specs=hbm,
        scratch_shapes=scratch,
        compiler_params=pltpu.CompilerParams(
            collective_id=0, has_side_effects=True, vmem_limit_bytes=60 * 1024 * 1024
        ),
    )(fields, sea_mask, partner, embed_weight, dw_weight, ln_gain, up_weight, down_weight)


def solution(mesh):
    in_specs = (
        P("lev", "gy", "gx"),
        P("gy", "gx"),
        P(),
        P("lev", None),
        P(None, "lev", None, None),
        P(None, "lev"),
        P(None, "lev", None),
        P(None, "lev", None),
    )
    out_specs = P("lev", "gy", "gx")
    return jax.shard_map(body, mesh=mesh, in_specs=in_specs, out_specs=out_specs, check_vma=False)
```

```python
import jax
import jax.numpy as jnp
from jax import lax
from jax.experimental import pallas as pl
from jax.experimental.pallas import tpu as pltpu
from jax.sharding import PartitionSpec as P

BF = jnp.bfloat16
F32 = jnp.float32
MESH = pl.DeviceIdType.MESH
GROUPS = 12


def twice_gelu(v):
    inner = v * (0.7978845608028654 + 0.035677408136300125 * (v * v))
    return v + v * jnp.tanh(inner)


def kernel(
    fields, sea, partner, embed, dw_weight, ln_gain, up, down,
    out,
    x_in, sea_in, partner_in, embed_in, dw_raw, gain_raw,
    xt, flat, pe, dw_in, dw_all, taps, end_taps, emb_t, w_own, w_other, down_t, gain, conv,
    state, south, north, diff, diff_s, diff_n, pack, from_w, from_e, xrow, edge_tile,
    fold_in, fold_out, fold_src, out_f, out_b, out_in,
    s_x, r_x, s_loc, s_w, r_w, s_halo, r_halo, s_f1, r_f1, s_f3, r_f3, s_o, r_o,
):
    lev = lax.axis_index("lev")
    x = lax.axis_index("gy")
    gx = lax.axis_index("gx")
    y = lev // 2
    h = lax.rem(lev, 2)
    t = gx // 2
    c = lax.rem(gx, 2)

    def row_block(yy):
        return jnp.where(lax.rem(x, 2) == 0, yy, 3 - yy)

    def half(hh):
        return lax.rem(hh + c, 2)

    def device(xx, yy, hh, tt, cc):
        return (yy * 2 + hh, xx, tt * 2 + cc)

    rb = row_block(y)
    s = half(h)
    col_block = (t * 2 + c) * 2 + s
    line = gx * 2 + h
    on_line = (x == 3) & (rb == 3)
    permutes = (x == 3) & (rb != 3) & (line < GROUPS)
    has_south = jnp.logical_not((x == 0) & (rb == 0))
    has_north = jnp.logical_not(on_line)

    outer_t = lax.rem(t + jnp.where(c == 0, 3, 1), 4)
    far = device(x, y, 1 - h, t, c)
    near = device(x, y, h, jnp.where(h == 0, outer_t, t), 1 - c)
    east_far = h == c
    east = tuple(jnp.where(east_far, f, n) for f, n in zip(far, near))
    west = tuple(jnp.where(east_far, n, f) for f, n in zip(far, near))
    step = jnp.where(lax.rem(x, 2) == 0, 1, -1)
    north_dev = device(
        jnp.where(rb == 3, jnp.minimum(x + 1, 3), x), jnp.where(rb == 3, y, jnp.clip(y + step, 0, 3)), h, t, c
    )
    south_dev = device(
        jnp.where(rb == 0, jnp.maximum(x - 1, 0), x), jnp.where(rb == 0, y, jnp.clip(y - step, 0, 3)), h, t, c
    )

    def remote(src, dst, send, recv, dev):
        return pltpu.make_async_remote_copy(
            src_ref=src, dst_ref=dst, send_sem=send, recv_sem=recv, device_id=dev, device_id_type=MESH
        )

    def arrived(dst, sem):
        remote(dst, dst, s_w.at[0], sem, far).wait_recv()

    ys = [lax.rem(y + k, 4) for k in range(4)]

    def cells_of(yy, hh):
        return (
            pl.ds(pl.multiple_of(row_block(yy) * 16, 16), 16),
            pl.ds(pl.multiple_of(half(hh) * 128, 128), 128),
        )

    my_rows, my_cols = cells_of(y, h)

    half_rows = pl.ds(pl.multiple_of(c * 48, 16), 48)
    slot = pe.at[y, h]
    dslot = dw_in.at[y, h]
    for k, ref in enumerate((up.at[0], down.at[0], up.at[1], down.at[1])):
        @pl.when(x == k)
        def _():
            pltpu.make_async_copy(ref.at[half_rows, :], slot.at[0], s_loc.at[0]).start()
    own = [
        pltpu.make_async_copy(embed, embed_in, s_loc.at[1]),
        pltpu.make_async_copy(dw_weight, dw_raw, s_loc.at[2]),
        pltpu.make_async_copy(ln_gain, gain_raw, s_loc.at[3]),
        pltpu.make_async_copy(sea.at[my_rows, my_cols], sea_in, s_loc.at[4]),
        pltpu.make_async_copy(partner, partner_in, s_loc.at[5]),
        pltpu.make_async_copy(fields.at[:, my_rows, my_cols], x_in.at[lev], s_loc.at[6]),
    ]
    for cp in own:
        cp.start()

    barrier = pltpu.get_barrier_semaphore()
    peers = [device(x, yy, 1 - h, t, c) for yy in ys]
    peers += [device(x, yy, h, t, c) for yy in ys[1:]]
    peers += [device(lax.rem(x + k, 4), y, h, t, c) for k in (1, 2, 3)]
    peers += [device(x, y, h, t, 1 - c)]

    def by_line(yy, p):
        return device(x, yy, lax.rem(p, 2), p // 4, lax.rem(p // 2, 2))

    def permuter(k, p):
        return by_line(1 + k, p)

    def rim_device(p):
        return by_line(0, p)

    def greet(dev):
        pl.semaphore_signal(barrier, inc=1, device_id=dev, device_id_type=MESH)

    for dev in peers:
        greet(dev)

    @pl.when(h == 0)
    def _():
        greet(near)

    @pl.when(on_line)
    def _():
        @pl.loop(0, GROUPS)
        def _(p):
            @pl.when(p // 2 != gx)
            def _():
                for k in range(3):
                    greet(permuter(k, p))

    @pl.when(permutes)
    def _():
        @pl.loop(0, 16)
        def _(p):
            @pl.when(p // 2 != gx)
            def _():
                greet(rim_device(p))

    own[0].wait()
    own[1].wait()
    own[2].wait()
    slot[1] = jnp.concatenate([embed_in[...].astype(F32), jnp.zeros((8, 192), F32)], axis=0).astype(BF)
    diagonal = lax.broadcasted_iota(jnp.int32, (24, 24), 0) == lax.broadcasted_iota(jnp.int32, (24, 24), 1)
    gains = gain_raw[...].astype(F32)
    for b in range(2):
        raw = jnp.concatenate([dw_raw[:, b, :], jnp.zeros((49, 104), F32)], axis=1)
        by_channel = jnp.concatenate([raw, jnp.zeros((79, 128), F32)], axis=0).T[:24, :]
        column = jnp.sum(jnp.where(diagonal, gains[b : b + 1, :], 0.0), axis=1, keepdims=True)
        dslot[b] = jnp.where(lax.broadcasted_iota(jnp.int32, (24, 128), 1) == 49, column, by_channel)
    pltpu.make_async_copy(up.at[0].at[half_rows, :], slot.at[0], s_loc.at[0]).wait()

    across = jnp.where(on_line, jnp.where(gx < 6, 30, 36), jnp.where(permutes, 14, 0))
    pl.semaphore_wait(barrier, len(peers) + 1 - h + across)

    sends = []

    def send(src, dst, send_sem, recv_sem, dev):
        cp = remote(src, dst, send_sem, recv_sem, dev)
        cp.start()
        sends.append(cp)

    send(slot, slot, s_w.at[0], r_w.at[0], far)
    send(dslot, dslot, s_w.at[1], r_w.at[1], far)

    others = [(k, 1) for k in range(4)] + [(k, 0) for k in range(1, 4)]
    for i, (k, flip) in enumerate(others):
        hh = lax.rem(h + flip, 2)
        rows, cols = cells_of(ys[k], hh)
        send(
            fields.at[:, rows, cols], x_in.at[lev], s_x.at[i], r_x.at[lev], device(x, ys[k], hh, t, c)
        )

    arrived(pe.at[y, 1 - h], r_w.at[0])
    arrived(dw_in.at[y, 1 - h], r_w.at[1])
    for k in (1, 2, 3):
        dev = device(x, ys[k], h, t, c)
        send(pe.at[y], pe.at[y], s_w.at[2 * k], r_w.at[2 + y], dev)
        send(dw_in.at[y], dw_in.at[y], s_w.at[2 * k + 1], r_w.at[6 + y], dev)

    own[4].wait()

    for k in (1, 2, 3):
        arrived(pe.at[ys[k]], r_w.at[2 + ys[k]])
        arrived(dw_in.at[ys[k]], r_w.at[6 + ys[k]])

    for k in (1, 2, 3):
        send(
            pe.at[:, :, 0], w_own.at[x], s_w.at[7 + k], r_w.at[10 + x], device(lax.rem(x + k, 4), y, h, t, c)
        )
    w_own[x] = pe[:, :, 0]
    for l in range(8):
        for b in range(2):
            dw_all[b, l * 24 : (l + 1) * 24, :] = dw_in[l // 2, l % 2, b]
    for b in range(2):
        gain[b] = jnp.broadcast_to(dw_all[b, :, 49:50], (192, 128))
    west16 = lax.rem(lax.broadcasted_iota(jnp.int32, (16, 128), 1), 6) >= 3
    for b in range(2):
        @pl.loop(0, GROUPS)
        def _(g):
            ch = pl.ds(pl.multiple_of(g * 16, 16), 16)
            row = dw_all[b, ch, :]
            wide = [jnp.broadcast_to(row[:, k : k + 1], (16, 128)) for k in range(49)]
            for k in range(49):
                taps[b, k, ch, :] = wide[k]
            for a in range(7):
                for d in range(3):
                    end_taps[b, a * 3 + d, ch, :] = jnp.where(west16, wide[a * 7 + d], wide[a * 7 + 4 + d])

    emb_t[...] = pe[:, :, 1].reshape(384, 192).astype(F32).T.astype(BF)
    for k in (1, 2, 3):
        xk = lax.rem(x + k, 4)
        arrived(w_own.at[xk], r_w.at[10 + xk])
    send(w_own, w_other, s_w.at[11], r_w.at[14], device(x, y, h, t, 1 - c))

    own[5].wait()
    for k, flip in [(0, 0)] + others[4:] + others[:4]:
        src = ys[k] * 2 + lax.rem(h + flip, 2)
        if (k, flip) != (0, 0):
            arrived(x_in.at[src], r_x.at[src])
        flat[...] = x_in[src].astype(F32).reshape(640, 128)
        place = pl.ds(pl.multiple_of(src * 48, 16), 48)

        @pl.loop(0, 16)
        def _(r):
            part = flat[pl.ds(r, 40, stride=16), :]
            xt[r, place, :] = jnp.concatenate([part, jnp.zeros((8, 128), F32)], axis=0).astype(BF)

    own[3].wait()

    def sea_rows(r):
        return sea_in[pl.ds(r, 1), :].astype(F32)

    lane = lax.broadcasted_iota(jnp.int32, (16, 128), 1)

    wide_lane = lax.broadcasted_iota(jnp.int32, (192, 128), 1)
    west_slot = lax.rem(wide_lane, 6) >= 3
    place = lax.rem(wide_lane, 3)
    row_ends = (wide_lane < 3) | (wide_lane >= 125)

    def group(g):
        return pl.ds(pl.multiple_of(g * 16, 16), 16)

    def rim_copy(b, k, tp, q):
        return remote(
            state.at[b, 15 - k, group(tp * 4 + q), :], fold_in.at[b, col_block],
            s_f1.at[b], r_f1.at[b], device(x, 1 + k, q % 2, tp, q // 2),
        )

    def ghost_copy(b, kind, tj, q):
        return remote(
            fold_out.at[b, kind, tj * 4 + q], north.at[b, kind, y - 1, group(line), :],
            s_f3.at[b, kind], r_f3.at[b, kind], device(x, 0, (q % 2) ^ (q // 2), tj, q // 2),
        )

    def row_copies(b):
        return (
            remote(state.at[b, pl.ds(13, 3)], south.at[b], s_halo.at[b, 0], r_halo.at[b, 0], north_dev),
            remote(state.at[b, pl.ds(0, 3)], north.at[b, 0], s_halo.at[b, 1], r_halo.at[b, 1], south_dev),
        )

    def side_copies(b):
        return (
            remote(diff.at[b], diff_s.at[b], s_halo.at[b, 4], r_halo.at[b, 4], north_dev),
            remote(diff.at[b], diff_n.at[b], s_halo.at[b, 5], r_halo.at[b, 5], south_dev),
        )

    def pack_copies(b):
        return (
            remote(pack.at[b], from_w.at[b], s_halo.at[b, 2], r_halo.at[b, 2], east),
            remote(pack.at[b], from_e.at[b], s_halo.at[b, 3], r_halo.at[b, 3], west),
        )

    def start_pair(pair):
        @pl.when(has_north)
        def _():
            pair[0].start()

        @pl.when(has_south)
        def _():
            pair[1].start()

    def rim_start(b):
        @pl.when(on_line)
        def _():
            @pl.loop(0, 3)
            def _(tp):
                for q in range(4):
                    for k in range(3):
                        rim_copy(b, k, tp, q).start()

    def halo_start(b):
        @pl.loop(0, 2)
        def _(g):
            ch = pl.ds(pl.multiple_of(g * 96, 96), 96)
            lane96 = lax.broadcasted_iota(jnp.int32, (96, 128), 1)
            tile = jnp.zeros((96, 128), F32)
            for r in range(16):
                v = state[b, r, ch, :].astype(F32)
                xrow[r + 3, ch, :] = v
                tile = jnp.where((lane96 >= 6 * r) & (lane96 < 6 * r + 6), pltpu.roll(v, 6 * r + 3, 1), tile)
            pack[b, ch, :] = tile.astype(BF)

        for cp in pack_copies(b):
            cp.start()
        start_pair(row_copies(b))

    def fold(b):
        arrived(fold_in.at[b], r_f1.at[b])
        for j in range(16):
            fold_src[j] = fold_in[b, j].astype(F32)

        @pl.loop(0, 4)
        def _(tj):
            for q in range(4):
                column = jnp.broadcast_to(partner_in[pl.ds(tj * 4 + q, 1), :], (16, 128))
                within, block = column & 127, column >> 7
                picked = [jnp.take_along_axis(fold_src[i], within, axis=1) for i in range(16)]
                for bit in range(4):
                    odd = ((block >> bit) & 1) == 1
                    picked = [jnp.where(odd, picked[i + 1], picked[i]) for i in range(0, len(picked), 2)]
                fold_out[b, 0, tj * 4 + q] = picked[0].astype(BF)
                ghost_copy(b, 0, tj, q).start()

        for j in range(16):
            after, before = fold_out[b, 0, (j + 1) % 16], fold_out[b, 0, (j + 15) % 16]
            fold_out[b, 1, j] = jnp.where(lane < 64, after.astype(F32), before.astype(F32)).astype(BF)

        @pl.loop(0, 4)
        def _(tj):
            for q in range(4):
                ghost_copy(b, 1, tj, q).start()

    def halo_middle(b):
        @pl.when(permutes)
        def _():
            fold(b)

        arrived(from_w.at[b], r_halo.at[b, 2])
        arrived(from_e.at[b], r_halo.at[b, 3])
        mine = pack[b].astype(F32)
        diff[b] = jnp.where(
            west_slot,
            pltpu.roll(from_w[b].astype(F32) - mine, 3, 1),
            pltpu.roll(from_e[b].astype(F32) - mine, 125, 1),
        )
        start_pair(side_copies(b))

    def south_in(b):
        @pl.when(has_south)
        def _():
            arrived(south.at[b], r_halo.at[b, 0])

        @pl.when(jnp.logical_not(has_south))
        def _():
            south[b] = jnp.zeros((3, 192, 128), BF)

    def south_sides_in(b):
        @pl.when(has_south)
        def _():
            arrived(diff_s.at[b], r_halo.at[b, 4])

        @pl.when(jnp.logical_not(has_south))
        def _():
            diff_s[b] = jnp.zeros((192, 128), F32)

    def north_in(b):
        @pl.when(has_north)
        def _():
            arrived(north.at[b, 0], r_halo.at[b, 1])

        @pl.when(on_line)
        def _():
            arrived(north.at[b, 0], r_f3.at[b, 0])

    def north_sides_in(b):
        @pl.when(has_north)
        def _():
            arrived(diff_n.at[b], r_halo.at[b, 5])

        @pl.when(on_line)
        def _():
            arrived(north.at[b, 1], r_f3.at[b, 1])

            @pl.loop(0, GROUPS)
            def _(g):
                ch = group(g)
                tile = jnp.zeros((16, 128), F32)
                for r in range(3):
                    d = north[b, 1, r, ch, :].astype(F32) - north[b, 0, r, ch, :].astype(F32)
                    tile = jnp.where((lane >= 6 * r) & (lane < 6 * r + 3), pltpu.roll(d, 6 * r, 1), tile)
                    tile = jnp.where(
                        (lane >= 6 * r + 3) & (lane < 6 * r + 6), pltpu.roll(d, 6 * r + 6, 1), tile
                    )
                diff_n[b, ch, :] = tile

    def halo_sent(b):
        for cp in pack_copies(b):
            cp.wait_send()

        for pair in (row_copies(b), side_copies(b)):
            @pl.when(has_north)
            def _():
                pair[0].wait_send()

            @pl.when(has_south)
            def _():
                pair[1].wait_send()

        @pl.when(on_line)
        def _():
            rim = state.at[b, pl.ds(13, 3)]
            remote(rim, rim, s_f1.at[b], r_f1.at[b], far).wait_send()

        @pl.when(permutes)
        def _():
            for kind in range(2):
                done = fold_out.at[b, kind]
                remote(done, done, s_f3.at[b, kind], r_f3.at[b, kind], far).wait_send()

    def depthwise(b, lo, count):
        @pl.loop(0, GROUPS)
        def _(g):
            ch = group(g)
            xs = [xrow[lo + r, ch, :] for r in range(count + 6)]
            acc = {}
            for e in range(7):
                w = [taps[b, a * 7 + e, ch, :] for a in range(7)]
                for q in range(count):
                    v = w[0] * xs[q]
                    for a in range(1, 7):
                        v = v + w[a] * xs[q + a]
                    if e != 3:
                        v = pltpu.roll(v, (3 - e) % 128, 1)
                    acc[q] = v if e == 0 else acc[q] + v
            for q in acc:
                conv[lo + q, ch, :] = acc[q]

    def correct(b, tile, lo, count):
        sums = [None] * 3
        for a in range(7):
            moved = pltpu.roll(tile, (-6 * a) % 128, 1) if a else tile
            for d in range(3):
                term = end_taps[b, a * 3 + d] * moved
                sums[d] = term if a == 0 else sums[d] + term
        fix = jnp.where(west_slot, sums[0], sums[2])
        fix = fix + jnp.where(west_slot & (place <= 1), pltpu.roll(sums[1], 127, 1), 0.0)
        fix = fix + jnp.where(~west_slot & (place >= 1), pltpu.roll(sums[1], 1, 1), 0.0)
        fix = fix + jnp.where(west_slot & (place == 0), pltpu.roll(sums[2], 126, 1), 0.0)
        fix = fix + jnp.where(~west_slot & (place == 2), pltpu.roll(sums[0], 2, 1), 0.0)
        for q in range(count):
            conv[lo + q] += jnp.where(row_ends, pltpu.roll(fix, (-6 * q - 3) % 128, 1), 0.0)

    def pointwise(b, first, part):
        parts = []
        for k in range(4):
            cv = conv[2 * first + k]
            mu = jnp.sum(cv, axis=0, keepdims=True) * (1.0 / 192)
            var = jnp.sum(cv * cv, axis=0, keepdims=True) * (1.0 / 192) - mu * mu
            parts.append(((cv - mu) * lax.rsqrt(var + 1e-6) * gain[b]).astype(BF))
        normed = jnp.concatenate(parts, axis=1)
        branch = jnp.zeros((192, 512), F32)
        for side, w in enumerate((w_own, w_other)):
            pre = jnp.dot(w[2 * b].reshape(384, 192), normed, preferred_element_type=F32)
            hidden = twice_gelu(pre.astype(BF))
            branch = branch + jnp.dot(down_t[b, side], hidden, preferred_element_type=F32)
        for k in range(4):
            r = 2 * first + k
            new = (state[b, r].astype(F32) + 0.5 * branch[:, k * 128 : (k + 1) * 128]) * sea_rows(r)
            state[b + 1, r] = new.astype(BF)
            out_f[pl.ds(part * 1536 + lax.rem(r, 8), 192, stride=8), :] = new

    def out_copy(part, i):
        k, flip = others[i]
        hh = lax.rem(h + flip, 2)
        chans = pl.ds((ys[k] * 2 + hh) * 12, 12)
        return remote(
            out_b.at[part, chans], out_in.at[part, lev], s_o.at[part, i], r_o.at[part, lev],
            device(x, ys[k], hh, t, c),
        )

    def out_start(part):
        def fill(l):
            rows = out_f[pl.ds(pl.multiple_of(part * 1536 + l * 192, 192), 192), :]
            out_b[part, pl.ds(l * 12, 12)] = rows.reshape(12, 16, 128).astype(BF)

        for i, (k, flip) in enumerate(others):
            fill(ys[k] * 2 + lax.rem(h + flip, 2))
            out_copy(part, i).start()
        fill(lev)
        out_in[part, lev] = out_b[part, pl.ds(lev * 12, 12)]

    @pl.loop(0, 4)
    def _(n):
        for q in range(2):
            r = 12 - 4 * n + 2 * q
            both = jnp.concatenate([xt[r], xt[r + 1]], axis=1)
            stem = jnp.dot(emb_t[...], both, preferred_element_type=F32)
            state[0, r] = (stem[:, :128] * sea_rows(r)).astype(BF)
            state[0, r + 1] = (stem[:, 128:] * sea_rows(r + 1)).astype(BF)

        @pl.when(n == 0)
        def _():
            rim_start(0)

    @pl.loop(0, 2)
    def _(b):
        halo_start(b)
        depthwise(b, 3, 10)

        @pl.when(b == 0)
        def _():
            arrived(w_other, r_w.at[14])

        for side, w in enumerate((w_own, w_other)):
            down_t[b, side] = w[2 * b + 1].reshape(384, 192).astype(F32).T.astype(BF)

        halo_middle(b)

        @pl.loop(0, 3)
        def _(phase):
            @pl.when(phase == 0)
            def _():
                correct(b, diff[b], 3, 10)

            @pl.when(phase == 1)
            def _():
                south_in(b)
                xrow[0:3] = south[b].astype(F32)

            @pl.when(phase == 2)
            def _():
                north_in(b)
                xrow[19:22] = north[b, 0].astype(F32)

            @pl.when(phase > 0)
            def _():
                lo = 13 * (phase - 1)
                depthwise(b, lo, 3)

                @pl.when(phase == 1)
                def _():
                    south_sides_in(b)
                    below = pltpu.roll(diff_s[b], 50, 1)
                    edge_tile[...] = jnp.where(wide_lane < 18, below, pltpu.roll(diff[b], 18, 1))

                @pl.when(phase == 2)
                def _():
                    north_sides_in(b)
                    above = pltpu.roll(diff_n[b], 36, 1)
                    edge_tile[...] = jnp.where(wide_lane < 36, pltpu.roll(diff[b], 68, 1), above)

                correct(b, edge_tile[...], lo, 3)

            @pl.loop(0, jnp.where(phase == 0, 2, 1))
            def _(n):
                pointwise(b, jnp.where(phase == 0, 2 + 2 * n, 6 * (phase - 1)), jnp.where(phase == 0, 0, 1))

            @pl.when((b == 0) & (phase == 2))
            def _():
                rim_start(1)

            @pl.when((b == 1) & (phase != 1))
            def _():
                out_start(phase // 2)

    upper = lax.broadcasted_iota(jnp.int32, (24, 8, 128), 1) < 4
    for k, flip in [(0, 0)] + others[4:] + others[:4]:
        hh = lax.rem(h + flip, 2)
        l = ys[k] * 2 + hh
        if (k, flip) != (0, 0):
            for part in range(2):
                arrived(out_in.at[part, l], r_o.at[part, l])
        mid = out_in[0, l].astype(F32).reshape(24, 8, 128)
        rim = out_in[1, l].astype(F32).reshape(24, 8, 128)
        rows, cols = cells_of(ys[k], hh)
        out[:, rows, cols] = jnp.concatenate(
            [jnp.where(upper, rim, mid), jnp.where(upper, mid, rim)], axis=1
        ).astype(BF)
    for part in range(2):
        for i in range(7):
            out_copy(part, i).wait_send()
    for cp in sends:
        cp.wait_send()
    @pl.loop(0, 2)
    def _(b):
        halo_sent(b)


def body(fields, sea_mask, fold_partner, embed_weight, dw_weight, ln_gain, up_weight, down_weight):
    partner = fold_partner.reshape(16, 128)
    by_tap = jnp.transpose(dw_weight, (2, 3, 0, 1)).reshape(49, 2, 24)
    hbm = pl.BlockSpec(memory_space=pl.ANY)
    dma = pltpu.SemaphoreType.DMA
    scratch = [
        pltpu.VMEM((8, 40, 16, 128), BF),
        pltpu.VMEM((16, 128), jnp.int32),
        pltpu.VMEM((16, 128), jnp.int32),
        pltpu.VMEM((40, 192), BF),
        pltpu.VMEM((49, 2, 24), F32),
        pltpu.VMEM((2, 24), BF),
        pltpu.VMEM((16, 384, 128), BF),
        pltpu.VMEM((640, 128), F32),
        pltpu.VMEM((4, 2, 2, 48, 192), BF),
        pltpu.VMEM((4, 2, 2, 24, 128), F32),
        pltpu.VMEM((2, 192, 128), F32),
        pltpu.VMEM((2, 49, 192, 128), F32),
        pltpu.VMEM((2, 21, 192, 128), F32),
        pltpu.VMEM((192, 384), BF),
        pltpu.VMEM((4, 4, 2, 48, 192), BF),
        pltpu.VMEM((4, 4, 2, 48, 192), BF),
        pltpu.VMEM((2, 2, 192, 384), BF),
        pltpu.VMEM((2, 192, 128), F32),
        pltpu.VMEM((16, 192, 128), F32),
        pltpu.VMEM((3, 16, 192, 128), BF),
        pltpu.VMEM((2, 3, 192, 128), BF),
        pltpu.VMEM((2, 2, 3, 192, 128), BF),
        pltpu.VMEM((2, 192, 128), F32),
        pltpu.VMEM((2, 192, 128), F32),
        pltpu.VMEM((2, 192, 128), F32),
        pltpu.VMEM((2, 192, 128), BF),
        pltpu.VMEM((2, 192, 128), BF),
        pltpu.VMEM((2, 192, 128), BF),
        pltpu.VMEM((22, 192, 128), F32),
        pltpu.VMEM((192, 128), F32),
        pltpu.VMEM((2, 16, 16, 128), BF),
        pltpu.VMEM((2, 2, 16, 16, 128), BF),
        pltpu.VMEM((16, 16, 128), F32),
        pltpu.VMEM((192 * 16, 128), F32),
        pltpu.VMEM((2, 96, 16, 128), BF),
        pltpu.VMEM((2, 8, 12, 16, 128), BF),
        dma((7,)), dma((8,)),
        dma((7,)),
        dma((12,)), dma((15,)),
        dma((2, 6)), dma((2, 6)),
        dma((2,)), dma((2,)),
        dma((2, 2)), dma((2, 2)),
        dma((2, 7)), dma((2, 8)),
    ]
    return pl.pallas_call(
        kernel,
        out_shape=jax.ShapeDtypeStruct((24, 64, 256), BF),
        in_specs=[hbm] * 8,
        out_specs=pl.BlockSpec(memory_space=pltpu.VMEM),
        scratch_shapes=scratch,
        compiler_params=pltpu.CompilerParams(
            collective_id=0, has_side_effects=True, vmem_limit_bytes=60 * 1024 * 1024
        ),
    )(fields, sea_mask, partner, embed_weight, by_tap, ln_gain, up_weight, down_weight)


def solution(mesh):
    in_specs = (
        P("lev", "gy", "gx"),
        P("gy", "gx"),
        P(),
        P("lev", None),
        P(None, "lev", None, None),
        P(None, "lev"),
        P(None, "lev", None),
        P(None, "lev", None),
    )
    out_specs = P("lev", "gy", "gx")
    return jax.shard_map(body, mesh=mesh, in_specs=in_specs, out_specs=out_specs, check_vma=False)
```

```python
import jax
import jax.numpy as jnp
from jax import lax
from jax.experimental import pallas as pl
from jax.experimental.pallas import tpu as pltpu
from jax.sharding import PartitionSpec as P

BF = jnp.bfloat16
F32 = jnp.float32
MESH = pl.DeviceIdType.MESH
GROUPS = 12


def twice_gelu(v):
    inner = v * (0.7978845608028654 + 0.035677408136300125 * (v * v))
    return v + v * jnp.tanh(inner)


def kernel(
    fields, sea, partner, embed, dw_weight, ln_gain, up, down,
    out,
    x_in, sea_in, partner_in, embed_in, dw_raw, gain_raw,
    xt, flat, pe, dw_in, dw_all, taps, end_taps, emb_t, w_own, w_other, down_t, gain, conv,
    state, south, north, diff, diff_s, diff_n, pack, from_w, from_e, xrow, edge_tile,
    fold_in, fold_out, fold_src, out_f, out_b, out_in,
    s_x, r_x, s_loc, s_w, r_w, s_halo, r_halo, s_f1, r_f1, s_f3, r_f3, s_o, r_o,
):
    lev = lax.axis_index("lev")
    x = lax.axis_index("gy")
    gx = lax.axis_index("gx")
    y = lev // 2
    h = lax.rem(lev, 2)
    t = gx // 2
    c = lax.rem(gx, 2)

    def row_block(yy):
        return jnp.where(lax.rem(x, 2) == 0, yy, 3 - yy)

    def half(hh):
        return lax.rem(hh + c, 2)

    def device(xx, yy, hh, tt, cc):
        return (yy * 2 + hh, xx, tt * 2 + cc)

    rb = row_block(y)
    s = half(h)
    col_block = (t * 2 + c) * 2 + s
    line = gx * 2 + h
    on_line = (x == 3) & (rb == 3)
    permutes = (x == 3) & (rb != 3) & (line < GROUPS)
    has_south = jnp.logical_not((x == 0) & (rb == 0))
    has_north = jnp.logical_not(on_line)

    outer_t = lax.rem(t + jnp.where(c == 0, 3, 1), 4)
    far = device(x, y, 1 - h, t, c)
    near = device(x, y, h, jnp.where(h == 0, outer_t, t), 1 - c)
    east_far = h == c
    east = tuple(jnp.where(east_far, f, n) for f, n in zip(far, near))
    west = tuple(jnp.where(east_far, n, f) for f, n in zip(far, near))
    step = jnp.where(lax.rem(x, 2) == 0, 1, -1)
    north_dev = device(
        jnp.where(rb == 3, jnp.minimum(x + 1, 3), x), jnp.where(rb == 3, y, jnp.clip(y + step, 0, 3)), h, t, c
    )
    south_dev = device(
        jnp.where(rb == 0, jnp.maximum(x - 1, 0), x), jnp.where(rb == 0, y, jnp.clip(y - step, 0, 3)), h, t, c
    )

    def remote(src, dst, send, recv, dev):
        return pltpu.make_async_remote_copy(
            src_ref=src, dst_ref=dst, send_sem=send, recv_sem=recv, device_id=dev, device_id_type=MESH
        )

    def arrived(dst, sem):
        remote(dst, dst, s_w.at[0], sem, far).wait_recv()

    ys = [lax.rem(y + k, 4) for k in range(4)]

    def cells_of(yy, hh):
        return (
            pl.ds(pl.multiple_of(row_block(yy) * 16, 16), 16),
            pl.ds(pl.multiple_of(half(hh) * 128, 128), 128),
        )

    my_rows, my_cols = cells_of(y, h)

    half_rows = pl.ds(pl.multiple_of(c * 48, 16), 48)
    slot = pe.at[y, h]
    dslot = dw_in.at[y, h]
    for k, ref in enumerate((up.at[0], down.at[0], up.at[1], down.at[1])):
        @pl.when(x == k)
        def _():
            pltpu.make_async_copy(ref.at[half_rows, :], slot.at[0], s_loc.at[0]).start()
    own = [
        pltpu.make_async_copy(embed, embed_in, s_loc.at[1]),
        pltpu.make_async_copy(dw_weight, dw_raw, s_loc.at[2]),
        pltpu.make_async_copy(ln_gain, gain_raw, s_loc.at[3]),
        pltpu.make_async_copy(sea.at[my_rows, my_cols], sea_in, s_loc.at[4]),
        pltpu.make_async_copy(partner, partner_in, s_loc.at[5]),
        pltpu.make_async_copy(fields.at[:, my_rows, my_cols], x_in.at[lev], s_loc.at[6]),
    ]
    for cp in own:
        cp.start()

    barrier = pltpu.get_barrier_semaphore()
    peers = [device(x, yy, 1 - h, t, c) for yy in ys]
    peers += [device(x, yy, h, t, c) for yy in ys[1:]]
    peers += [device(lax.rem(x + k, 4), y, h, t, c) for k in (1, 2, 3)]
    peers += [device(x, y, h, t, 1 - c)]

    def by_line(yy, p):
        return device(x, yy, lax.rem(p, 2), p // 4, lax.rem(p // 2, 2))

    def permuter(k, p):
        return by_line(1 + k, p)

    def rim_device(p):
        return by_line(0, p)

    def greet(dev):
        pl.semaphore_signal(barrier, inc=1, device_id=dev, device_id_type=MESH)

    for dev in peers:
        greet(dev)

    @pl.when(h == 0)
    def _():
        greet(near)

    @pl.when(on_line)
    def _():
        @pl.loop(0, GROUPS)
        def _(p):
            @pl.when(p // 2 != gx)
            def _():
                for k in range(3):
                    greet(permuter(k, p))

    @pl.when(permutes)
    def _():
        @pl.loop(0, 16)
        def _(p):
            @pl.when(p // 2 != gx)
            def _():
                greet(rim_device(p))

    own[0].wait()
    own[1].wait()
    own[2].wait()
    slot[1] = jnp.concatenate([embed_in[...].astype(F32), jnp.zeros((8, 192), F32)], axis=0).astype(BF)
    diagonal = lax.broadcasted_iota(jnp.int32, (24, 24), 0) == lax.broadcasted_iota(jnp.int32, (24, 24), 1)
    gains = gain_raw[...].astype(F32)
    for b in range(2):
        raw = jnp.concatenate([dw_raw[:, b, :], jnp.zeros((49, 104), F32)], axis=1)
        by_channel = jnp.concatenate([raw, jnp.zeros((79, 128), F32)], axis=0).T[:24, :]
        column = jnp.sum(jnp.where(diagonal, gains[b : b + 1, :], 0.0), axis=1, keepdims=True)
        dslot[b] = jnp.where(lax.broadcasted_iota(jnp.int32, (24, 128), 1) == 49, column, by_channel)
    pltpu.make_async_copy(up.at[0].at[half_rows, :], slot.at[0], s_loc.at[0]).wait()

    across = jnp.where(on_line, jnp.where(gx < 6, 30, 36), jnp.where(permutes, 14, 0))
    pl.semaphore_wait(barrier, len(peers) + 1 - h + across)

    sends = []

    def send(src, dst, send_sem, recv_sem, dev):
        cp = remote(src, dst, send_sem, recv_sem, dev)
        cp.start()
        sends.append(cp)

    send(slot, slot, s_w.at[0], r_w.at[0], far)
    send(dslot, dslot, s_w.at[1], r_w.at[1], far)

    others = [(k, 1) for k in range(4)] + [(k, 0) for k in range(1, 4)]
    for i, (k, flip) in enumerate(others):
        hh = lax.rem(h + flip, 2)
        rows, cols = cells_of(ys[k], hh)
        send(
            fields.at[:, rows, cols], x_in.at[lev], s_x.at[i], r_x.at[lev], device(x, ys[k], hh, t, c)
        )

    arrived(pe.at[y, 1 - h], r_w.at[0])
    arrived(dw_in.at[y, 1 - h], r_w.at[1])
    for k in (1, 2, 3):
        dev = device(x, ys[k], h, t, c)
        send(pe.at[y], pe.at[y], s_w.at[2 * k], r_w.at[2 + y], dev)
        send(dw_in.at[y], dw_in.at[y], s_w.at[2 * k + 1], r_w.at[6 + y], dev)

    own[4].wait()

    for k in (1, 2, 3):
        arrived(pe.at[ys[k]], r_w.at[2 + ys[k]])
        arrived(dw_in.at[ys[k]], r_w.at[6 + ys[k]])

    for k in (1, 2, 3):
        send(
            pe.at[:, :, 0], w_own.at[x], s_w.at[7 + k], r_w.at[10 + x], device(lax.rem(x + k, 4), y, h, t, c)
        )
    w_own[x] = pe[:, :, 0]
    for l in range(8):
        for b in range(2):
            dw_all[b, l * 24 : (l + 1) * 24, :] = dw_in[l // 2, l % 2, b]
    for b in range(2):
        gain[b] = jnp.broadcast_to(dw_all[b, :, 49:50], (192, 128))
    west16 = lax.rem(lax.broadcasted_iota(jnp.int32, (16, 128), 1), 6) >= 3
    for b in range(2):
        @pl.loop(0, GROUPS)
        def _(g):
            ch = pl.ds(pl.multiple_of(g * 16, 16), 16)
            row = dw_all[b, ch, :]
            wide = [jnp.broadcast_to(row[:, k : k + 1], (16, 128)) for k in range(49)]
            for k in range(49):
                taps[b, k, ch, :] = wide[k]
            for a in range(7):
                for d in range(3):
                    end_taps[b, a * 3 + d, ch, :] = jnp.where(west16, wide[a * 7 + d], wide[a * 7 + 4 + d])

    emb_t[...] = pe[:, :, 1].reshape(384, 192).astype(F32).T.astype(BF)
    own[5].wait()
    for k, flip in [(0, 0)] + others[4:] + others[:4]:
        src = ys[k] * 2 + lax.rem(h + flip, 2)
        if (k, flip) != (0, 0):
            arrived(x_in.at[src], r_x.at[src])
        flat[...] = x_in[src].astype(F32).reshape(640, 128)
        place = pl.ds(pl.multiple_of(src * 48, 16), 48)

        @pl.loop(0, 16)
        def _(r):
            part = flat[pl.ds(r, 40, stride=16), :]
            xt[r, place, :] = jnp.concatenate([part, jnp.zeros((8, 128), F32)], axis=0).astype(BF)

    own[3].wait()

    def sea_rows(r):
        return sea_in[pl.ds(r, 1), :].astype(F32)

    lane = lax.broadcasted_iota(jnp.int32, (16, 128), 1)

    wide_lane = lax.broadcasted_iota(jnp.int32, (192, 128), 1)
    west_slot = lax.rem(wide_lane, 6) >= 3
    place = lax.rem(wide_lane, 3)
    row_ends = (wide_lane < 3) | (wide_lane >= 125)

    def group(g):
        return pl.ds(pl.multiple_of(g * 16, 16), 16)

    def rim_copy(b, k, tp, q):
        return remote(
            state.at[b, 15 - k, group(tp * 4 + q), :], fold_in.at[b, col_block],
            s_f1.at[b], r_f1.at[b], device(x, 1 + k, q % 2, tp, q // 2),
        )

    def ghost_copy(b, kind, tj, q):
        return remote(
            fold_out.at[b, kind, tj * 4 + q], north.at[b, kind, y - 1, group(line), :],
            s_f3.at[b, kind], r_f3.at[b, kind], device(x, 0, (q % 2) ^ (q // 2), tj, q // 2),
        )

    def row_copies(b):
        return (
            remote(state.at[b, pl.ds(13, 3)], south.at[b], s_halo.at[b, 0], r_halo.at[b, 0], north_dev),
            remote(state.at[b, pl.ds(0, 3)], north.at[b, 0], s_halo.at[b, 1], r_halo.at[b, 1], south_dev),
        )

    def side_copies(b):
        return (
            remote(diff.at[b], diff_s.at[b], s_halo.at[b, 4], r_halo.at[b, 4], north_dev),
            remote(diff.at[b], diff_n.at[b], s_halo.at[b, 5], r_halo.at[b, 5], south_dev),
        )

    def pack_copies(b):
        return (
            remote(pack.at[b], from_w.at[b], s_halo.at[b, 2], r_halo.at[b, 2], east),
            remote(pack.at[b], from_e.at[b], s_halo.at[b, 3], r_halo.at[b, 3], west),
        )

    def start_pair(pair):
        @pl.when(has_north)
        def _():
            pair[0].start()

        @pl.when(has_south)
        def _():
            pair[1].start()

    def rim_start(b):
        @pl.when(on_line)
        def _():
            @pl.loop(0, 3)
            def _(tp):
                for q in range(4):
                    for k in range(3):
                        rim_copy(b, k, tp, q).start()

    def halo_start(b):
        @pl.loop(0, 2)
        def _(g):
            ch = pl.ds(pl.multiple_of(g * 96, 96), 96)
            lane96 = lax.broadcasted_iota(jnp.int32, (96, 128), 1)
            tile = jnp.zeros((96, 128), F32)
            for r in range(16):
                v = state[b, r, ch, :].astype(F32)
                xrow[r + 3, ch, :] = v
                tile = jnp.where((lane96 >= 6 * r) & (lane96 < 6 * r + 6), pltpu.roll(v, 6 * r + 3, 1), tile)
            pack[b, ch, :] = tile.astype(BF)

        for cp in pack_copies(b):
            cp.start()
        start_pair(row_copies(b))

    def fold(b):
        arrived(fold_in.at[b], r_f1.at[b])
        for j in range(16):
            fold_src[j] = fold_in[b, j].astype(F32)

        @pl.loop(0, 4)
        def _(tj):
            for q in range(4):
                column = jnp.broadcast_to(partner_in[pl.ds(tj * 4 + q, 1), :], (16, 128))
                within, block = column & 127, column >> 7
                picked = [jnp.take_along_axis(fold_src[i], within, axis=1) for i in range(16)]
                for bit in range(4):
                    odd = ((block >> bit) & 1) == 1
                    picked = [jnp.where(odd, picked[i + 1], picked[i]) for i in range(0, len(picked), 2)]
                fold_out[b, 0, tj * 4 + q] = picked[0].astype(BF)
                ghost_copy(b, 0, tj, q).start()

        for j in range(16):
            after, before = fold_out[b, 0, (j + 1) % 16], fold_out[b, 0, (j + 15) % 16]
            fold_out[b, 1, j] = jnp.where(lane < 64, after.astype(F32), before.astype(F32)).astype(BF)

        @pl.loop(0, 4)
        def _(tj):
            for q in range(4):
                ghost_copy(b, 1, tj, q).start()

    def halo_middle(b):
        @pl.when(permutes)
        def _():
            fold(b)

        arrived(from_w.at[b], r_halo.at[b, 2])
        arrived(from_e.at[b], r_halo.at[b, 3])
        mine = pack[b].astype(F32)
        diff[b] = jnp.where(
            west_slot,
            pltpu.roll(from_w[b].astype(F32) - mine, 3, 1),
            pltpu.roll(from_e[b].astype(F32) - mine, 125, 1),
        )
        start_pair(side_copies(b))

    def south_in(b):
        @pl.when(has_south)
        def _():
            arrived(south.at[b], r_halo.at[b, 0])

        @pl.when(jnp.logical_not(has_south))
        def _():
            south[b] = jnp.zeros((3, 192, 128), BF)

    def south_sides_in(b):
        @pl.when(has_south)
        def _():
            arrived(diff_s.at[b], r_halo.at[b, 4])

        @pl.when(jnp.logical_not(has_south))
        def _():
            diff_s[b] = jnp.zeros((192, 128), F32)

    def north_in(b):
        @pl.when(has_north)
        def _():
            arrived(north.at[b, 0], r_halo.at[b, 1])

        @pl.when(on_line)
        def _():
            arrived(north.at[b, 0], r_f3.at[b, 0])

    def north_sides_in(b):
        @pl.when(has_north)
        def _():
            arrived(diff_n.at[b], r_halo.at[b, 5])

        @pl.when(on_line)
        def _():
            arrived(north.at[b, 1], r_f3.at[b, 1])

            @pl.loop(0, GROUPS)
            def _(g):
                ch = group(g)
                tile = jnp.zeros((16, 128), F32)
                for r in range(3):
                    d = north[b, 1, r, ch, :].astype(F32) - north[b, 0, r, ch, :].astype(F32)
                    tile = jnp.where((lane >= 6 * r) & (lane < 6 * r + 3), pltpu.roll(d, 6 * r, 1), tile)
                    tile = jnp.where(
                        (lane >= 6 * r + 3) & (lane < 6 * r + 6), pltpu.roll(d, 6 * r + 6, 1), tile
                    )
                diff_n[b, ch, :] = tile

    def halo_sent(b):
        for cp in pack_copies(b):
            cp.wait_send()

        for pair in (row_copies(b), side_copies(b)):
            @pl.when(has_north)
            def _():
                pair[0].wait_send()

            @pl.when(has_south)
            def _():
                pair[1].wait_send()

        @pl.when(on_line)
        def _():
            rim = state.at[b, pl.ds(13, 3)]
            remote(rim, rim, s_f1.at[b], r_f1.at[b], far).wait_send()

        @pl.when(permutes)
        def _():
            for kind in range(2):
                done = fold_out.at[b, kind]
                remote(done, done, s_f3.at[b, kind], r_f3.at[b, kind], far).wait_send()

    def depthwise(b, lo, count):
        @pl.loop(0, GROUPS)
        def _(g):
            ch = group(g)
            xs = [xrow[lo + r, ch, :] for r in range(count + 6)]
            acc = {}
            for e in range(7):
                w = [taps[b, a * 7 + e, ch, :] for a in range(7)]
                for q in range(count):
                    v = w[0] * xs[q]
                    for a in range(1, 7):
                        v = v + w[a] * xs[q + a]
                    if e != 3:
                        v = pltpu.roll(v, (3 - e) % 128, 1)
                    acc[q] = v if e == 0 else acc[q] + v
            for q in acc:
                conv[lo + q, ch, :] = acc[q]

    def correct(b, tile, lo, count):
        sums = [None] * 3
        for a in range(7):
            moved = pltpu.roll(tile, (-6 * a) % 128, 1) if a else tile
            for d in range(3):
                term = end_taps[b, a * 3 + d] * moved
                sums[d] = term if a == 0 else sums[d] + term
        fix = jnp.where(west_slot, sums[0], sums[2])
        fix = fix + jnp.where(west_slot & (place <= 1), pltpu.roll(sums[1], 127, 1), 0.0)
        fix = fix + jnp.where(~west_slot & (place >= 1), pltpu.roll(sums[1], 1, 1), 0.0)
        fix = fix + jnp.where(west_slot & (place == 0), pltpu.roll(sums[2], 126, 1), 0.0)
        fix = fix + jnp.where(~west_slot & (place == 2), pltpu.roll(sums[0], 2, 1), 0.0)
        for q in range(count):
            conv[lo + q] += jnp.where(row_ends, pltpu.roll(fix, (-6 * q - 3) % 128, 1), 0.0)

    def pointwise(b, first, part):
        parts = []
        for k in range(4):
            cv = conv[2 * first + k]
            mu = jnp.sum(cv, axis=0, keepdims=True) * (1.0 / 192)
            var = jnp.sum(cv * cv, axis=0, keepdims=True) * (1.0 / 192) - mu * mu
            parts.append(((cv - mu) * lax.rsqrt(var + 1e-6) * gain[b]).astype(BF))
        normed = jnp.concatenate(parts, axis=1)
        branch = jnp.zeros((192, 512), F32)
        for side, w in enumerate((w_own, w_other)):
            pre = jnp.dot(w[2 * b].reshape(384, 192), normed, preferred_element_type=F32)
            hidden = twice_gelu(pre.astype(BF))
            branch = branch + jnp.dot(down_t[b, side], hidden, preferred_element_type=F32)
        for k in range(4):
            r = 2 * first + k
            new = (state[b, r].astype(F32) + 0.5 * branch[:, k * 128 : (k + 1) * 128]) * sea_rows(r)
            state[b + 1, r] = new.astype(BF)
            out_f[pl.ds(part * 1536 + lax.rem(r, 8), 192, stride=8), :] = new

    def out_copy(part, i):
        k, flip = others[i]
        hh = lax.rem(h + flip, 2)
        chans = pl.ds((ys[k] * 2 + hh) * 12, 12)
        return remote(
            out_b.at[part, chans], out_in.at[part, lev], s_o.at[part, i], r_o.at[part, lev],
            device(x, ys[k], hh, t, c),
        )

    def out_start(part):
        def fill(l):
            rows = out_f[pl.ds(pl.multiple_of(part * 1536 + l * 192, 192), 192), :]
            out_b[part, pl.ds(l * 12, 12)] = rows.reshape(12, 16, 128).astype(BF)

        for i, (k, flip) in enumerate(others):
            fill(ys[k] * 2 + lax.rem(h + flip, 2))
            out_copy(part, i).start()
        fill(lev)
        out_in[part, lev] = out_b[part, pl.ds(lev * 12, 12)]

    @pl.loop(0, 4)
    def _(n):
        for q in range(2):
            r = 12 - 4 * n + 2 * q
            both = jnp.concatenate([xt[r], xt[r + 1]], axis=1)
            stem = jnp.dot(emb_t[...], both, preferred_element_type=F32)
            state[0, r] = (stem[:, :128] * sea_rows(r)).astype(BF)
            state[0, r + 1] = (stem[:, 128:] * sea_rows(r + 1)).astype(BF)

        @pl.when(n == 0)
        def _():
            rim_start(0)

    for k in (1, 2, 3):
        xk = lax.rem(x + k, 4)
        arrived(w_own.at[xk], r_w.at[10 + xk])
    send(w_own, w_other, s_w.at[11], r_w.at[14], device(x, y, h, t, 1 - c))

    @pl.loop(0, 2)
    def _(b):
        halo_start(b)
        depthwise(b, 3, 10)

        @pl.when(b == 0)
        def _():
            arrived(w_other, r_w.at[14])

        for side, w in enumerate((w_own, w_other)):
            down_t[b, side] = w[2 * b + 1].reshape(384, 192).astype(F32).T.astype(BF)

        halo_middle(b)

        @pl.loop(0, 3)
        def _(phase):
            @pl.when(phase == 0)
            def _():
                correct(b, diff[b], 3, 10)

            @pl.when(phase == 1)
            def _():
                south_in(b)
                xrow[0:3] = south[b].astype(F32)

            @pl.when(phase == 2)
            def _():
                north_in(b)
                xrow[19:22] = north[b, 0].astype(F32)

            @pl.when(phase > 0)
            def _():
                lo = 13 * (phase - 1)
                depthwise(b, lo, 3)

                @pl.when(phase == 1)
                def _():
                    south_sides_in(b)
                    below = pltpu.roll(diff_s[b], 50, 1)
                    edge_tile[...] = jnp.where(wide_lane < 18, below, pltpu.roll(diff[b], 18, 1))

                @pl.when(phase == 2)
                def _():
                    north_sides_in(b)
                    above = pltpu.roll(diff_n[b], 36, 1)
                    edge_tile[...] = jnp.where(wide_lane < 36, pltpu.roll(diff[b], 68, 1), above)

                correct(b, edge_tile[...], lo, 3)

            @pl.loop(0, jnp.where(phase == 0, 2, 1))
            def _(n):
                pointwise(b, jnp.where(phase == 0, 2 + 2 * n, 6 * (phase - 1)), jnp.where(phase == 0, 0, 1))

            @pl.when((b == 0) & (phase == 2))
            def _():
                rim_start(1)

            @pl.when((b == 1) & (phase != 1))
            def _():
                out_start(phase // 2)

    upper = lax.broadcasted_iota(jnp.int32, (24, 8, 128), 1) < 4
    for k, flip in [(0, 0)] + others[4:] + others[:4]:
        hh = lax.rem(h + flip, 2)
        l = ys[k] * 2 + hh
        if (k, flip) != (0, 0):
            for part in range(2):
                arrived(out_in.at[part, l], r_o.at[part, l])
        mid = out_in[0, l].astype(F32).reshape(24, 8, 128)
        rim = out_in[1, l].astype(F32).reshape(24, 8, 128)
        rows, cols = cells_of(ys[k], hh)
        out[:, rows, cols] = jnp.concatenate(
            [jnp.where(upper, rim, mid), jnp.where(upper, mid, rim)], axis=1
        ).astype(BF)
    for part in range(2):
        for i in range(7):
            out_copy(part, i).wait_send()
    for cp in sends:
        cp.wait_send()
    @pl.loop(0, 2)
    def _(b):
        halo_sent(b)


def body(fields, sea_mask, fold_partner, embed_weight, dw_weight, ln_gain, up_weight, down_weight):
    partner = fold_partner.reshape(16, 128)
    by_tap = jnp.transpose(dw_weight, (2, 3, 0, 1)).reshape(49, 2, 24)
    hbm = pl.BlockSpec(memory_space=pl.ANY)
    dma = pltpu.SemaphoreType.DMA
    scratch = [
        pltpu.VMEM((8, 40, 16, 128), BF),
        pltpu.VMEM((16, 128), jnp.int32),
        pltpu.VMEM((16, 128), jnp.int32),
        pltpu.VMEM((40, 192), BF),
        pltpu.VMEM((49, 2, 24), F32),
        pltpu.VMEM((2, 24), BF),
        pltpu.VMEM((16, 384, 128), BF),
        pltpu.VMEM((640, 128), F32),
        pltpu.VMEM((4, 2, 2, 48, 192), BF),
        pltpu.VMEM((4, 2, 2, 24, 128), F32),
        pltpu.VMEM((2, 192, 128), F32),
        pltpu.VMEM((2, 49, 192, 128), F32),
        pltpu.VMEM((2, 21, 192, 128), F32),
        pltpu.VMEM((192, 384), BF),
        pltpu.VMEM((4, 4, 2, 48, 192), BF),
        pltpu.VMEM((4, 4, 2, 48, 192), BF),
        pltpu.VMEM((2, 2, 192, 384), BF),
        pltpu.VMEM((2, 192, 128), F32),
        pltpu.VMEM((16, 192, 128), F32),
        pltpu.VMEM((3, 16, 192, 128), BF),
        pltpu.VMEM((2, 3, 192, 128), BF),
        pltpu.VMEM((2, 2, 3, 192, 128), BF),
        pltpu.VMEM((2, 192, 128), F32),
        pltpu.VMEM((2, 192, 128), F32),
        pltpu.VMEM((2, 192, 128), F32),
        pltpu.VMEM((2, 192, 128), BF),
        pltpu.VMEM((2, 192, 128), BF),
        pltpu.VMEM((2, 192, 128), BF),
        pltpu.VMEM((22, 192, 128), F32),
        pltpu.VMEM((192, 128), F32),
        pltpu.VMEM((2, 16, 16, 128), BF),
        pltpu.VMEM((2, 2, 16, 16, 128), BF),
        pltpu.VMEM((16, 16, 128), F32),
        pltpu.VMEM((192 * 16, 128), F32),
        pltpu.VMEM((2, 96, 16, 128), BF),
        pltpu.VMEM((2, 8, 12, 16, 128), BF),
        dma((7,)), dma((8,)),
        dma((7,)),
        dma((12,)), dma((15,)),
        dma((2, 6)), dma((2, 6)),
        dma((2,)), dma((2,)),
        dma((2, 2)), dma((2, 2)),
        dma((2, 7)), dma((2, 8)),
    ]
    return pl.pallas_call(
        kernel,
        out_shape=jax.ShapeDtypeStruct((24, 64, 256), BF),
        in_specs=[hbm] * 8,
        out_specs=pl.BlockSpec(memory_space=pltpu.VMEM),
        scratch_shapes=scratch,
        compiler_params=pltpu.CompilerParams(
            collective_id=0, has_side_effects=True, vmem_limit_bytes=60 * 1024 * 1024
        ),
    )(fields, sea_mask, partner, embed_weight, by_tap, ln_gain, up_weight, down_weight)


def solution(mesh):
    in_specs = (
        P("lev", "gy", "gx"),
        P("gy", "gx"),
        P(),
        P("lev", None),
        P(None, "lev", None, None),
        P(None, "lev"),
        P(None, "lev", None),
        P(None, "lev", None),
    )
    out_specs = P("lev", "gy", "gx")
    return jax.shard_map(body, mesh=mesh, in_specs=in_specs, out_specs=out_specs, check_vma=False)
```
